32 devices in a mesh: dp: 8 (over z, x), expert: 4 (over y, core).
Axes of the slice: x: 2, y: 2, z: 4, core: 2. Of those that a mesh axis runs over, the one named last changes fastest.
Arguments:
- grad_output: bfloat16 [512, 6144], P('expert', 'dp'), may hold values from -6 to 6
- gate_probs: float32 [512, 4], P('expert'), may hold values from 0.05 to 1
- routing: int32 [512, 4], P('expert'), may hold values from 0 to 15, all different within a row; in each aligned block of 128 rows (0 to 127, 128 to 255, ...) at most 40 rows name the same one
- old_weights: bfloat16 [16, 1024, 6144], P('expert', None, 'dp'), may hold values from -0.1875 to 0.1875
- old_slot_expert: int32 [16], replicated, may hold values from 0 to 15, each once
- new_slot_expert: int32 [16], replicated, may hold values from 0 to 15, each once
- saved_hidden: bfloat16 [16, 160, 1024], P('expert'), may hold values from -6 to 6
- shared_hidden: bfloat16 [512, 1024], P('expert'), may hold values from -6 to 6
- shared_weight: bfloat16 [1024, 6144], P('expert', 'dp'), may hold values from -0.1875 to 0.1875
Outputs:
- expert_weight_grad: bfloat16 [16, 1024, 6144], P('expert', None, 'dp')
- expert_hidden_grad: bfloat16 [16, 160, 1024], P('expert', 'dp')
- shared_hidden_grad: bfloat16 [512, 1024], P('expert', 'dp')
- shared_weight_grad: bfloat16 [1024, 6144], P('expert', 'dp')
The draws below stay inside these ranges and needn't reach their ends.
Inputs may be any that keep to these rules, and one draw needn't show every extreme that they name: `routing`: each row names 4 different experts. Among the 128 rows of one group no expert is named by more than 40 rows, a bound that some block reaches of them. `old_slot_expert`: A permutation of the experts. `new_slot_expert`: A permutation of the experts.
All inputs are finite; a program needn't handle non-finite values.
Results may differ from the reference program's by a relative error of at most 0.023.
Values may be sent and summed in bfloat16 or wider, within the bound.
A program may use at most 64 MiB of HBM per device.

```python
import math
import jax
import jax.numpy as jnp
import numpy as np
from jax import lax

D = 6144
FF_E = 1024
HS = 1024
TOP = 4
TOK_GRP = 128
EXPERTS = 16
CAP = 40
TOKENS = 512
N_DP = 8
N_EXPERT = 4


def block_scale(rng, extent, shards, smallest, largest):
    def one(dim, blocks):
        draws = jax.random.uniform(jax.random.fold_in(jax.random.fold_in(rng, 6), dim), (blocks,), jnp.float32, smallest / len(shards), largest / len(shards))
        return jnp.repeat(jnp.exp(draws), extent[dim] // blocks).reshape((-1,) + (1,) * (len(extent) - dim - 1))

    factor_of = one(*shards[0])
    for cut in shards[1:]:
        factor_of = factor_of * one(*cut)
    return factor_of


def shared_out(own_key, own, number, rows, amount, top, bound, skew):
    order = jax.random.permutation(own_key, amount)
    packed, ordinary = portions_of(amount, rows * top, bound, skew, True), portions_of(amount, rows * top, bound, skew, False)
    places = jnp.arange(amount)

    def named(tallies, rotation):
        used = int((tallies > 0).sum())
        fixed = max(1, used // 4)
        shifted = fixed + (places - fixed + rotation * (used - fixed)) % max(1, amount - fixed)
        return jnp.zeros((amount,), jnp.int32).at[order[jnp.where(places < fixed, places, shifted)]].set(jnp.asarray(tallies, jnp.int32))

    tallies = jnp.where(number % 4 == 0, named(packed, number // 4), named(ordinary, number - number // 4 - 1))
    mixed = jax.random.permutation(jax.random.fold_in(own, 3), amount)
    source_of, taker = mixed[0:amount // 2 * 2:2], mixed[1:amount // 2 * 2:2]
    room = jnp.minimum(tallies[source_of] - 1, bound - tallies[taker]) // 2
    room = jnp.where((source_of == order[0]) | (taker == order[0]) | (tallies[taker] == 0), 0, jnp.maximum(room, 0))
    shifted = jax.random.randint(jax.random.fold_in(own, 4), (amount // 2,), 0, 1 << 20) % (room + 1)
    tallies = tallies.at[source_of].add(-shifted).at[taker].add(shifted)
    items = jnp.searchsorted(jnp.cumsum(tallies), jnp.arange(rows * top), side="right").astype(jnp.int32)
    table = items.reshape(top, rows).T
    table = table[jax.random.permutation(jax.random.fold_in(own, 1), rows)]
    rotation = jax.random.randint(jax.random.fold_in(own, 2), (rows, 1), 0, top)
    return jnp.take_along_axis(table, (jnp.arange(top)[None, :] + rotation) % top, axis=1)


def portions_of(number_of, total, bound, lean, full):
    portions = [(1 << 20) // math.isqrt(rank ** lean) + 1 for rank in range(1, number_of + 1)]
    largest = bound if full else min(bound, max(-(-total // number_of), total * portions[0] // sum(portions)))
    least = 1 if total - largest >= number_of - 1 else 0
    holding, surplus = [largest] + [least] * (number_of - 1), total - largest - least * (number_of - 1)
    while surplus > 0:
        candidates = [i for i in range(1, number_of) if holding[i] < largest] or [i for i in range(1, number_of) if holding[i] < bound]
        whole, remaining = sum([portions[i] for i in candidates]), surplus
        for i in candidates:
            more = min(bound - holding[i], max(1, remaining * portions[i] // whole), surplus)
            holding[i] = holding[i] + more
            surplus = surplus - more
    return np.array(holding)


def bell_draw(own_key, extent, deviation, reach, pieces=(), kind=jnp.bfloat16):
    result = deviation * jax.random.normal(own_key, extent, jnp.float32)
    if pieces:
        result = result * block_scale(own_key, extent, pieces, -0.22, 0.18)
    return jnp.clip(result, -reach, reach).astype(kind)


def setup_inputs(seed: int = 0) -> dict:
    arg_keys = jax.random.split(jax.random.key(seed), 10)
    grad_output = bell_draw(arg_keys[0], (TOKENS, D), 1.0, 6.0, ((0, 4), (1, 8)))
    gate_probs = jnp.clip(jnp.exp(math.log(1.0) - 2.9957323 * jax.random.uniform(arg_keys[1], (TOKENS, TOP), jnp.float32) ** block_scale(arg_keys[1], (TOKENS, TOP), ((0, 4),), -0.2, 0.2)), 0.05, 1.0)
    routing_keys = jax.random.split(jax.random.fold_in(arg_keys[2], 1), TOKENS // TOK_GRP)
    routing_turns = jax.random.permutation(jax.random.fold_in(arg_keys[2], 3), TOKENS // TOK_GRP)
    routing = jax.vmap(lambda own, number: shared_out(jax.random.fold_in(arg_keys[2], 2), own, number, TOK_GRP, EXPERTS, TOP, CAP, 2))(routing_keys, routing_turns).reshape((TOKENS, TOP))
    old_weights = bell_draw(arg_keys[3], (EXPERTS, FF_E, D), FF_E ** -0.5, 0.1875, ((0, 4), (2, 8)))
    old_slot_expert = jax.random.permutation(arg_keys[4], EXPERTS).astype(jnp.int32)
    new_slot_expert = jax.random.permutation(arg_keys[5], EXPERTS).astype(jnp.int32)
    saved_hidden = bell_draw(arg_keys[6], (EXPERTS, N_EXPERT * CAP, FF_E), 1.0, 6.0, ((0, 4),))
    shared_hidden = bell_draw(arg_keys[7], (TOKENS, HS), 1.0, 6.0, ((0, 4),))
    shared_weight = bell_draw(arg_keys[8], (HS, D), HS ** -0.5, 0.1875, ((0, 4), (1, 8)))
    return {"grad_output": grad_output, "gate_probs": gate_probs, "routing": routing, "old_weights": old_weights, "old_slot_expert": old_slot_expert, "new_slot_expert": new_slot_expert, "saved_hidden": saved_hidden, "shared_hidden": shared_hidden, "shared_weight": shared_weight}


def inverse_order(listing):
    labels = jnp.arange(listing.shape[0], dtype=jnp.int32)
    return jnp.sum(jnp.where(listing[None, :] == labels[:, None], labels[None, :], 0), axis=1).astype(jnp.int32)


def reference(grad_output, gate_probs, routing, old_weights, old_slot_expert, new_slot_expert, saved_hidden, shared_hidden, shared_weight):
    experts, hidden, columns = old_weights.shape
    slot_rows = saved_hidden.shape[1]
    capacity = slot_rows // N_EXPERT
    tokens, chosen = routing.shape
    tok_grp = tokens // N_EXPERT
    shared_units = shared_weight.shape[0]
    blocksize = columns // N_DP
    old_position = inverse_order(old_slot_expert)
    new_position = inverse_order(new_slot_expert)
    source_slot = jnp.take(old_position, new_slot_expert).astype(jnp.int32)
    relayed = jnp.take(old_weights, source_slot, axis=0)
    labels = jnp.arange(experts, dtype=jnp.int32)
    flattened = routing.reshape(N_EXPERT, tok_grp * chosen)
    onehot = (flattened[:, :, None] == labels[None, None, :]).astype(jnp.int32)
    earlier = jnp.cumsum(onehot, axis=1) - onehot
    ranking = jnp.sum(earlier * onehot, axis=2).astype(jnp.int32)
    slot_index = jnp.take(new_position, flattened.reshape(-1)).reshape(N_EXPERT, tok_grp * chosen).astype(jnp.int32)
    sources = jnp.arange(N_EXPERT, dtype=jnp.int32)[:, None]
    target = (slot_index * slot_rows + sources * capacity + ranking).reshape(-1).astype(jnp.int32)
    scaled = (grad_output.astype(jnp.float32)[:, None, :] * gate_probs[:, :, None]).astype(jnp.bfloat16).reshape(tokens * chosen, columns)
    routed_rows = jnp.zeros((experts * slot_rows, columns), jnp.bfloat16).at[target].set(scaled).reshape(experts, slot_rows, columns)

    def one_expert(operands):
        incoming, weight, saved = operands
        weight_grad = jnp.dot(saved.T, incoming, preferred_element_type=jnp.float32).astype(jnp.bfloat16)
        partial_value = jnp.einsum("rbc,fbc->brf", incoming.reshape(slot_rows, N_DP, blocksize).astype(jnp.float32), weight.reshape(hidden, N_DP, blocksize).astype(jnp.float32))
        rounded = lax.optimization_barrier(partial_value.astype(jnp.bfloat16)).astype(jnp.float32)
        return weight_grad, jnp.sum(rounded, axis=0).astype(jnp.bfloat16)

    expert_weight_grad, expert_hidden_grad = lax.map(one_expert, (routed_rows, relayed, saved_hidden))

    grad_blocks = jnp.transpose(grad_output.reshape(tokens, N_DP, blocksize), (1, 0, 2))
    weight_blocks = jnp.transpose(shared_weight.reshape(shared_units, N_DP, blocksize), (1, 0, 2))

    def add_block(total, operands):
        grad_part, weight_part = operands
        term = jnp.dot(grad_part, weight_part.T, preferred_element_type=jnp.float32)
        rounded = lax.optimization_barrier(term.astype(jnp.bfloat16)).astype(jnp.float32)
        return total + rounded, None

    shared_total, _ = lax.scan(add_block, jnp.zeros((tokens, shared_units), jnp.float32), (grad_blocks, weight_blocks))
    shared_hidden_grad = shared_total.astype(jnp.bfloat16)

    hidden_groups = shared_hidden.reshape(N_EXPERT, tok_grp, shared_units)
    grad_groups = grad_output.reshape(N_EXPERT, tok_grp, columns)

    def add_group(total, operands):
        hidden_part, grad_part = operands
        term = jnp.dot(hidden_part.T, grad_part, preferred_element_type=jnp.float32)
        rounded = lax.optimization_barrier(term.astype(jnp.bfloat16)).astype(jnp.float32)
        return total + rounded, None

    weight_total, _ = lax.scan(add_group, jnp.zeros((shared_units, columns), jnp.float32), (hidden_groups, grad_groups))
    shared_weight_grad = weight_total.astype(jnp.bfloat16)
    return expert_weight_grad, expert_hidden_grad, shared_hidden_grad, shared_weight_grad
```

```python
import functools

import jax
import jax.numpy as jnp
from jax import lax
from jax.experimental import pallas as pl
from jax.experimental.pallas import tpu as pltpu
from jax.sharding import PartitionSpec as P

MESH = pl.DeviceIdType.MESH
F32 = jnp.float32
BF16 = jnp.bfloat16
CHUNKS = 4


def remote(src, dst, send, recv, device):
    return pltpu.make_async_remote_copy(
        src_ref=src, dst_ref=dst, send_sem=send, recv_sem=recv, device_id=device, device_id_type=MESH
    )


def exchange_kernel(
    n_dp,
    n_ex,
    sliced,
    grad_ref,
    table_ref,
    old_ref,
    new_ref,
    hidden_ref,
    shared_ref,
    weights_hbm,
    rows_ref,
    routed_ref,
    hidden_grad_ref,
    weight_grad_ref,
    weights,
    grads,
    tables,
    hiddens,
    shareds,
    picked,
    product,
    stage,
    part,
    part_in,
    pair_sum,
    ring_in,
    total,
    gathered,
    spart,
    spart_in,
    spair_sum,
    sring_in,
    local_sem,
    table_sem,
    grad_sem,
    grad_pair_sem,
    shared_sem,
    shared_pair_sem,
    hidden_sem,
    pair_sem,
    ring_sem,
    spread_sem,
):
    d, g = lax.axis_index("dp"), lax.axis_index("expert")
    n_z, n_y = n_dp // 2, n_ex // 2
    z, x = d // 2, lax.rem(d, 2)
    y, c = g // 2, lax.rem(g, 2)
    local, slot_rows, columns = rows_ref.shape
    cap = slot_rows // n_ex
    tok = grad_ref.shape[0]
    tokens = tok * n_ex
    chosen = table_ref.shape[0] // 2
    piece = slot_rows // n_dp
    hidden = weights.shape[1]
    width = hidden // CHUNKS

    def pair_of(first):
        return (d, first * 2 + (1 - c))

    def line_dest(dy):
        return lax.rem(y + dy, n_y) * 2 + c

    def line_source(dy):
        return lax.rem(y + n_y - dy, n_y) * 2 + c

    loads = []
    for k in range(CHUNKS):
        cut = pl.ds(k * width, width)
        loads.append(
            pltpu.make_async_copy(weights_hbm.at[:, cut], weights.at[:, cut], local_sem.at[k])
        )
        loads[-1].start()

    barrier = pltpu.get_barrier_semaphore()
    peers = [(d, lax.rem(g + k, n_ex)) for k in range(1, n_ex)]
    peers += [(z * 2 + (1 - x), g)]
    peers += [(lax.rem(z + k, n_z) * 2 + x, g) for k in range(1, n_z)]
    for peer in peers:
        pl.semaphore_signal(barrier, inc=1, device_id=peer, device_id_type=MESH)
    pl.semaphore_wait(barrier, len(peers))

    sent = []

    def send(copy):
        copy.start()
        sent.append(copy)

    def gather_start(ref, buffer, sem, pair):
        for k in range(1, n_y):
            send(remote(ref, buffer.at[g], sem.at[0, k], sem.at[1, k], (d, line_dest(k))))
        send(remote(ref, buffer.at[g], pair.at[0, 0], pair.at[1, 0], (d, y * 2 + (1 - c))))

    def gather_forward(ref, buffer, sem, pair):
        for k in range(1, n_y):
            source = line_source(k)
            remote(ref, buffer.at[source], sem.at[0, k], sem.at[1, k], (d, source)).wait_recv()
            block = buffer.at[source]
            send(remote(block, block, pair.at[0, k], pair.at[1, k], (d, y * 2 + (1 - c))))

    def gather_end(ref, buffer, sem, pair):
        for k in range(n_y):
            source = lax.rem(y + n_y - k, n_y) * 2 + (1 - c)
            remote(ref, buffer.at[source], pair.at[0, k], pair.at[1, k], (d, source)).wait_recv()

    for k in range(1, n_ex):
        peer = lax.rem(g + k, n_ex)
        send(remote(table_ref, tables.at[g], table_sem.at[0, k], table_sem.at[1, k], (d, peer)))
    gather_start(grad_ref, grads, grad_sem, grad_pair_sem)
    tables[g] = table_ref[...]
    grads[g] = grad_ref[...]
    shareds[g] = shared_ref[...]
    unit = hiddens.shape[2]

    def hidden_piece(owner):
        if sliced:
            return hidden_ref.at[:, pl.ds(pl.multiple_of(owner * unit, unit), unit)]
        return hidden_ref.at[owner]

    if sliced:
        hiddens[g] = hidden_ref[:, pl.ds(pl.multiple_of(g * unit, unit), unit)]
    else:
        hiddens[g] = hidden_ref[g]

    for k in range(1, n_ex):
        source = lax.rem(g + n_ex - k, n_ex)
        remote(
            table_ref, tables.at[source], table_sem.at[0, k], table_sem.at[1, k], (d, source)
        ).wait_recv()
    place = lax.broadcasted_iota(jnp.int32, (2 * local, 1), 0)
    labels = jnp.zeros((2 * local, 1), F32)
    for s in range(local):
        labels = jnp.where(place == s, old_ref[g * local + s].astype(F32), labels)
        labels = jnp.where(place == local + s, new_ref[g * local + s].astype(F32), labels)
    before = (
        lax.broadcasted_iota(jnp.int32, (tok, tok), 0)
        < lax.broadcasted_iota(jnp.int32, (tok, tok), 1)
    ).astype(BF16)
    codes, gates = [], []
    for p in range(n_ex):
        table = tables[p]
        named = jnp.zeros((2 * local, tok), F32)
        gate = jnp.zeros((2 * local, tok), F32)
        for k in range(chosen):
            hit = table[k : k + 1, :] == labels
            named = jnp.where(hit, 1.0, named)
            gate = jnp.where(hit, table[chosen + k : chosen + k + 1, :], gate)
        rank = jnp.dot(named.astype(BF16), before, preferred_element_type=F32)
        codes.append(jnp.where(named > 0, rank + float(p * cap), -1.0))
        gates.append(gate)
    code = jnp.concatenate(codes, axis=1)
    gate = jnp.concatenate(gates, axis=1)
    row = lax.broadcasted_iota(jnp.int32, (slot_rows, tokens), 0).astype(F32)

    def build(s, tokens_in):
        hit = code[s : s + 1, :] == row
        scale = jnp.sum(jnp.where(hit, gate[s : s + 1, :], 0.0), axis=1, keepdims=True)
        chosen_rows = jnp.dot(hit.astype(BF16), tokens_in, preferred_element_type=F32)
        return (chosen_rows * scale).astype(BF16)

    gather_forward(grad_ref, grads, grad_sem, grad_pair_sem)
    gather_start(shared_ref, shareds, shared_sem, shared_pair_sem)
    for k in range(1, n_ex):
        peer = lax.rem(g + k, n_ex)
        send(
            remote(
                hidden_piece(peer), hiddens.at[g], hidden_sem.at[0, k], hidden_sem.at[1, k], (d, peer)
            )
        )
    gather_end(grad_ref, grads, grad_sem, grad_pair_sem)
    all_tokens = grads[...].reshape(tokens, columns)

    for s in range(local):
        picked[s] = build(s, all_tokens)

    def pair_send(k, source, target):
        send(
            remote(
                source.at[1 - x], target, pair_sem.at[0, k], pair_sem.at[1, k], (z * 2 + (1 - x), g)
            )
        )

    for k in range(CHUNKS):
        loads[k].wait()
        for s in range(local):
            product[...] = lax.dot_general(
                picked[s],
                weights[s, k * width : (k + 1) * width, :],
                (((1,), (1,)), ((), ())),
                preferred_element_type=F32,
            )
            for t in range(n_dp):
                stage[t, s * piece : (s + 1) * piece, :] = product[t * piece : (t + 1) * piece, :]
        for t in range(n_dp):
            part[k, t % 2, t // 2] = stage[t].astype(BF16)
        pair_send(k, part.at[k], part_in.at[k])

    gather_forward(shared_ref, shareds, shared_sem, shared_pair_sem)
    for s in range(local):
        rows_ref[s] = build(local + s, all_tokens)
    gather_end(shared_ref, shareds, shared_sem, shared_pair_sem)
    units = shared_ref.shape[0] * n_ex
    shared_all = shareds[...].reshape(units, columns)
    share = units // n_dp
    for t in range(n_dp):
        spart[t % 2, t // 2] = lax.dot_general(
            grad_ref[...],
            shared_all[t * share : (t + 1) * share, :],
            (((1,), (1,)), ((), ())),
            preferred_element_type=F32,
        ).astype(BF16)
    pair_send(CHUNKS, spart, spart_in)

    def ring_start(k, own, arrived, sums, landing):
        remote(
            own.at[x], arrived, pair_sem.at[0, k], pair_sem.at[1, k], (z * 2 + (1 - x), g)
        ).wait_recv()
        sums[...] = (own[x].astype(F32) + arrived[...].astype(F32)).astype(BF16)
        for step in range(1, n_z):
            to = lax.rem(z + step, n_z)
            send(
                remote(
                    sums.at[to],
                    landing.at[step - 1],
                    ring_sem.at[0, k, step],
                    ring_sem.at[1, k, step],
                    (to * 2 + x, g),
                )
            )

    def ring_end(k, sums, landing):
        result = sums[z].astype(F32)
        for step in range(1, n_z):
            source = lax.rem(z + n_z - step, n_z)
            remote(
                sums.at[z],
                landing.at[step - 1],
                ring_sem.at[0, k, step],
                ring_sem.at[1, k, step],
                (source * 2 + x, g),
            ).wait_recv()
            result = result + landing[step - 1].astype(F32)
        return result.astype(BF16)

    for k in range(CHUNKS):
        ring_start(k, part.at[k], part_in.at[k], pair_sum.at[k], ring_in.at[k])
        if k == 1:
            for j in range(1, n_ex):
                source = lax.rem(g + n_ex - j, n_ex)
                remote(
                    hidden_piece(source),
                    hiddens.at[source],
                    hidden_sem.at[0, j],
                    hidden_sem.at[1, j],
                    (d, source),
                ).wait_recv()
            weight_grad_ref[...] = lax.dot_general(
                hiddens[...].reshape(tokens, unit),
                all_tokens,
                (((0,), (0,)), ((), ())),
                preferred_element_type=F32,
            ).astype(BF16)
    ring_start(CHUNKS, spart, spart_in, spair_sum, sring_in)

    for k in range(CHUNKS):
        total[k] = ring_end(k, pair_sum.at[k], ring_in.at[k])
        gathered[k, g] = total[k]
        for j in range(1, n_ex):
            send(
                remote(
                    total.at[k],
                    gathered.at[k, g],
                    spread_sem.at[0, k, j],
                    spread_sem.at[1, k, j],
                    (d, lax.rem(g + j, n_ex)),
                )
            )
    hidden_grad_ref[...] = ring_end(CHUNKS, spair_sum, sring_in)

    high = lax.broadcasted_iota(jnp.int32, (piece, local * piece), 0)
    wide = lax.broadcasted_iota(jnp.int32, (piece, local * piece), 1)
    for k in range(CHUNKS):
        for j in range(1, n_ex):
            source = lax.rem(g + n_ex - j, n_ex)
            remote(
                total.at[k],
                gathered.at[k, source],
                spread_sem.at[0, k, j],
                spread_sem.at[1, k, j],
                (d, source),
            ).wait_recv()
        for s in range(local):
            wanted = new_ref[g * local + s]
            found = jnp.zeros((piece, width), F32)
            for p in range(n_ex):
                choice = jnp.zeros((piece, local * piece), F32)
                for q in range(local):
                    same = jnp.where(old_ref[p * local + q] == wanted, 1.0, 0.0)
                    choice = jnp.where(wide == high + q * piece, same, choice)
                found = found + jnp.dot(
                    choice.astype(BF16), gathered[k, p], preferred_element_type=F32
                )
            routed_ref[s, :, k * width : (k + 1) * width] = found.astype(BF16)

    for copy in sent:
        copy.wait_send()


def weight_grad_kernel(saved_ref, rows_ref, out_ref):
    out_ref[0] = lax.dot_general(
        saved_ref[0], rows_ref[0], (((0,), (0,)), ((), ())), preferred_element_type=F32
    ).astype(BF16)


def on_device(
    n_dp,
    n_ex,
    grad_output,
    gate_probs,
    routing,
    old_weights,
    old_slot_expert,
    new_slot_expert,
    saved_hidden,
    shared_hidden,
    shared_weight,
):
    local, hidden, columns = old_weights.shape
    slot_rows = saved_hidden.shape[1]
    tok = grad_output.shape[0]
    units_here = shared_weight.shape[0]
    units = shared_hidden.shape[1]
    table = jnp.concatenate([routing.T.astype(F32), gate_probs.T], axis=0)
    sliced = units_here % 128 == 0
    if not sliced:
        shared_hidden = shared_hidden.reshape(tok, n_ex, units_here).transpose(1, 0, 2)
    piece = slot_rows // n_dp
    packed = local * piece
    width = hidden // CHUNKS
    share = units // n_dp
    n_z, n_y = n_dp // 2, n_ex // 2
    vmem = pl.BlockSpec(memory_space=pltpu.VMEM)
    smem = pl.BlockSpec(memory_space=pltpu.SMEM)
    sem = pltpu.SemaphoreType.DMA
    rows, routed, hidden_grad, weight_grad = pl.pallas_call(
        functools.partial(exchange_kernel, n_dp, n_ex, sliced),
        out_shape=(
            jax.ShapeDtypeStruct((local, slot_rows, columns), BF16),
            jax.ShapeDtypeStruct((local, piece, hidden), BF16),
            jax.ShapeDtypeStruct((tok, share), BF16),
            jax.ShapeDtypeStruct((units_here, columns), BF16),
        ),
        in_specs=[vmem, vmem, smem, smem, vmem, vmem, pl.BlockSpec(memory_space=pl.ANY)],
        out_specs=(vmem, vmem, vmem, vmem),
        scratch_shapes=[
            pltpu.VMEM((local, hidden, columns), BF16),
            pltpu.VMEM((n_ex, tok, columns), BF16),
            pltpu.VMEM((n_ex,) + table.shape, F32),
            pltpu.VMEM((n_ex, tok, units_here), BF16),
            pltpu.VMEM((n_ex, units_here, columns), BF16),
            pltpu.VMEM((local, slot_rows, columns), BF16),
            pltpu.VMEM((slot_rows, width), F32),
            pltpu.VMEM((n_dp, packed, width), F32),
            pltpu.VMEM((CHUNKS, 2, n_z, packed, width), BF16),
            pltpu.VMEM((CHUNKS, n_z, packed, width), BF16),
            pltpu.VMEM((CHUNKS, n_z, packed, width), BF16),
            pltpu.VMEM((CHUNKS, n_z - 1, packed, width), BF16),
            pltpu.VMEM((CHUNKS, packed, width), BF16),
            pltpu.VMEM((CHUNKS, n_ex, packed, width), BF16),
            pltpu.VMEM((2, n_z, tok, share), BF16),
            pltpu.VMEM((n_z, tok, share), BF16),
            pltpu.VMEM((n_z, tok, share), BF16),
            pltpu.VMEM((n_z - 1, tok, share), BF16),
            sem((CHUNKS,)),
            sem((2, n_ex)),
            sem((2, n_y)),
            sem((2, n_y)),
            sem((2, n_y)),
            sem((2, n_y)),
            sem((2, n_ex)),
            sem((2, CHUNKS + 1)),
            sem((2, CHUNKS + 1, n_z)),
            sem((2, CHUNKS, n_ex)),
        ],
        compiler_params=pltpu.CompilerParams(
            collective_id=0, has_side_effects=True, vmem_limit_bytes=48 * 1024 * 1024
        ),
    )(grad_output, table, old_slot_expert, new_slot_expert, shared_hidden, shared_weight, old_weights)
    splits = 2
    expert_weight_grad = pl.pallas_call(
        weight_grad_kernel,
        out_shape=jax.ShapeDtypeStruct((local, hidden, columns), BF16),
        grid=(local, splits),
        in_specs=[
            pl.BlockSpec((1, slot_rows, hidden // splits), lambda i, j: (i, 0, j)),
            pl.BlockSpec((1, slot_rows, columns), lambda i, j: (i, 0, 0)),
        ],
        out_specs=pl.BlockSpec((1, hidden // splits, columns), lambda i, j: (i, j, 0)),
    )(saved_hidden, rows)
    return expert_weight_grad, routed, hidden_grad, weight_grad


def solution(mesh):
    return jax.shard_map(
        functools.partial(on_device, mesh.shape["dp"], mesh.shape["expert"]),
        mesh=mesh,
        in_specs=(
            P("expert", "dp"),
            P("expert", None),
            P("expert", None),
            P("expert", None, "dp"),
            P(),
            P(),
            P("expert", None, None),
            P("expert", None),
            P("expert", "dp"),
        ),
        out_specs=(
            P("expert", None, "dp"),
            P("expert", "dp", None),
            P("expert", "dp"),
            P("expert", "dp"),
        ),
        check_vma=False,
    )
```

```python
import functools

import jax
import jax.numpy as jnp
from jax import lax
from jax.experimental import pallas as pl
from jax.experimental.pallas import tpu as pltpu
from jax.sharding import PartitionSpec as P

MESH = pl.DeviceIdType.MESH
F32 = jnp.float32
BF16 = jnp.bfloat16
CHUNKS = 4


def remote(src, dst, send, recv, device):
    return pltpu.make_async_remote_copy(
        src_ref=src, dst_ref=dst, send_sem=send, recv_sem=recv, device_id=device, device_id_type=MESH
    )


def exchange_kernel(
    n_dp,
    n_ex,
    sliced,
    grad_ref,
    route_ref,
    gate_ref,
    old_hbm,
    new_hbm,
    hidden_ref,
    shared_ref,
    weights_hbm,
    saved_hbm,
    expert_grad_hbm,
    routed_ref,
    hidden_grad_ref,
    weight_grad_ref,
    old_ref,
    new_ref,
    weights,
    saved,
    expert_grad,
    rows,
    grads,
    routes,
    gate_tables,
    hiddens,
    shareds,
    picked,
    product,
    stage,
    part,
    part_in,
    pair_sum,
    ring_in,
    total,
    gathered,
    spart,
    spart_in,
    spair_sum,
    sring_in,
    local_sem,
    own_sem,
    out_sem,
    route_sem,
    gate_sem,
    grad_sem,
    grad_pair_sem,
    shared_sem,
    shared_pair_sem,
    hidden_sem,
    pair_sem,
    ring_sem,
    spread_sem,
):
    d, g = lax.axis_index("dp"), lax.axis_index("expert")
    n_z, n_y = n_dp // 2, n_ex // 2
    z, x = d // 2, lax.rem(d, 2)
    y, c = g // 2, lax.rem(g, 2)
    local, slot_rows, columns = rows.shape
    cap = slot_rows // n_ex
    tok = grad_ref.shape[0]
    tokens = tok * n_ex
    chosen = route_ref.shape[0]
    piece = slot_rows // n_dp
    hidden = weights.shape[1]
    width = hidden // CHUNKS

    def pair_of(first):
        return (d, first * 2 + (1 - c))

    def line_dest(dy):
        return lax.rem(y + dy, n_y) * 2 + c

    def line_source(dy):
        return lax.rem(y + n_y - dy, n_y) * 2 + c

    unit = hiddens.shape[2]

    def hidden_piece(owner):
        if sliced:
            return hidden_ref.at[:, pl.ds(pl.multiple_of(owner * unit, unit), unit)]
        return hidden_ref.at[owner]

    own = [
        (old_hbm, old_ref),
        (new_hbm, new_ref),
        (route_ref, routes.at[g]),
        (gate_ref, gate_tables.at[g]),
        (grad_ref, grads.at[g]),
        (shared_ref, shareds.at[g]),
        (hidden_piece(g), hiddens.at[g]),
        (saved_hbm, saved),
    ]
    own = [pltpu.make_async_copy(a, b, own_sem.at[i]) for i, (a, b) in enumerate(own)]
    for copy in own:
        copy.start()
    loads = []
    for k in range(CHUNKS):
        cut = pl.ds(k * width, width)
        loads.append(
            pltpu.make_async_copy(weights_hbm.at[:, cut], weights.at[:, cut], local_sem.at[k])
        )
        loads[-1].start()

    barrier = pltpu.get_barrier_semaphore()
    peers = [(d, lax.rem(g + k, n_ex)) for k in range(1, n_ex)]
    peers += [(z * 2 + (1 - x), g)]
    peers += [(lax.rem(z + k, n_z) * 2 + x, g) for k in range(1, n_z)]
    for peer in peers:
        pl.semaphore_signal(barrier, inc=1, device_id=peer, device_id_type=MESH)
    pl.semaphore_wait(barrier, len(peers))

    sent = []

    def send(copy):
        copy.start()
        sent.append(copy)

    def gather_start(ref, buffer, sem, pair):
        for k in range(1, n_y):
            send(remote(ref, buffer.at[g], sem.at[0, k], sem.at[1, k], (d, line_dest(k))))
        send(remote(ref, buffer.at[g], pair.at[0, 0], pair.at[1, 0], (d, y * 2 + (1 - c))))

    def gather_forward(ref, buffer, sem, pair):
        for k in range(1, n_y):
            source = line_source(k)
            remote(ref, buffer.at[source], sem.at[0, k], sem.at[1, k], (d, source)).wait_recv()
            block = buffer.at[source]
            send(remote(block, block, pair.at[0, k], pair.at[1, k], (d, y * 2 + (1 - c))))

    def gather_end(ref, buffer, sem, pair):
        for k in range(n_y):
            source = lax.rem(y + n_y - k, n_y) * 2 + (1 - c)
            remote(ref, buffer.at[source], pair.at[0, k], pair.at[1, k], (d, source)).wait_recv()

    for k in range(1, n_ex):
        peer = lax.rem(g + k, n_ex)
        send(remote(route_ref, routes.at[g], route_sem.at[0, k], route_sem.at[1, k], (d, peer)))
        send(remote(gate_ref, gate_tables.at[g], gate_sem.at[0, k], gate_sem.at[1, k], (d, peer)))
    gather_start(grad_ref, grads, grad_sem, grad_pair_sem)

    for k in range(1, n_ex):
        source = lax.rem(g + n_ex - k, n_ex)
        remote(
            route_ref, routes.at[source], route_sem.at[0, k], route_sem.at[1, k], (d, source)
        ).wait_recv()
        remote(
            gate_ref, gate_tables.at[source], gate_sem.at[0, k], gate_sem.at[1, k], (d, source)
        ).wait_recv()
    for copy in own[:4]:
        copy.wait()
    place = lax.broadcasted_iota(jnp.int32, (2 * local, 1), 0)
    labels = jnp.zeros((2 * local, 1), F32)
    for s in range(local):
        labels = jnp.where(place == s, old_ref[g * local + s].astype(F32), labels)
        labels = jnp.where(place == local + s, new_ref[g * local + s].astype(F32), labels)
    before = (
        lax.broadcasted_iota(jnp.int32, (tok, tok), 0)
        < lax.broadcasted_iota(jnp.int32, (tok, tok), 1)
    ).astype(BF16)
    codes, gates = [], []
    for p in range(n_ex):
        table, gate_table = routes[p].astype(F32), gate_tables[p]
        named = jnp.zeros((2 * local, tok), F32)
        gate = jnp.zeros((2 * local, tok), F32)
        for k in range(chosen):
            hit = table[k : k + 1, :] == labels
            named = jnp.where(hit, 1.0, named)
            gate = jnp.where(hit, gate_table[k : k + 1, :], gate)
        rank = jnp.dot(named.astype(BF16), before, preferred_element_type=F32)
        codes.append(jnp.where(named > 0, rank + float(p * cap), -1.0))
        gates.append(gate)
    code = jnp.concatenate(codes, axis=1)
    gate = jnp.concatenate(gates, axis=1)
    row = lax.broadcasted_iota(jnp.int32, (slot_rows, tokens), 0).astype(F32)

    def build(s, tokens_in):
        hit = code[s : s + 1, :] == row
        scale = jnp.sum(jnp.where(hit, gate[s : s + 1, :], 0.0), axis=1, keepdims=True)
        chosen_rows = jnp.dot(hit.astype(BF16), tokens_in, preferred_element_type=F32)
        return (chosen_rows * scale).astype(BF16)

    gather_forward(grad_ref, grads, grad_sem, grad_pair_sem)
    gather_start(shared_ref, shareds, shared_sem, shared_pair_sem)
    for k in range(1, n_ex):
        peer = lax.rem(g + k, n_ex)
        send(
            remote(
                hidden_piece(peer), hiddens.at[g], hidden_sem.at[0, k], hidden_sem.at[1, k], (d, peer)
            )
        )
    gather_end(grad_ref, grads, grad_sem, grad_pair_sem)
    own[4].wait()
    all_tokens = grads[...].reshape(tokens, columns)

    for s in range(local):
        picked[s] = build(s, all_tokens)

    def pair_send(k, source, target):
        send(
            remote(
                source.at[1 - x], target, pair_sem.at[0, k], pair_sem.at[1, k], (z * 2 + (1 - x), g)
            )
        )

    for k in range(CHUNKS):
        loads[k].wait()
        for s in range(local):
            product[...] = lax.dot_general(
                picked[s],
                weights[s, k * width : (k + 1) * width, :],
                (((1,), (1,)), ((), ())),
                preferred_element_type=F32,
            )
            for t in range(n_dp):
                stage[t, s * piece : (s + 1) * piece, :] = product[t * piece : (t + 1) * piece, :]
        for t in range(n_dp):
            part[k, t % 2, t // 2] = stage[t].astype(BF16)
        pair_send(k, part.at[k], part_in.at[k])

    gather_forward(shared_ref, shareds, shared_sem, shared_pair_sem)
    for s in range(local):
        rows[s] = build(local + s, all_tokens)
    gather_end(shared_ref, shareds, shared_sem, shared_pair_sem)
    own[5].wait()
    units = shared_ref.shape[0] * n_ex
    shared_all = shareds[...].reshape(units, columns)
    share = units // n_dp
    own_tokens = grads[g]
    for t in range(n_dp):
        spart[t % 2, t // 2] = lax.dot_general(
            own_tokens,
            shared_all[t * share : (t + 1) * share, :],
            (((1,), (1,)), ((), ())),
            preferred_element_type=F32,
        ).astype(BF16)
    pair_send(CHUNKS, spart, spart_in)

    def ring_start(k, own, arrived, sums, landing):
        remote(
            own.at[x], arrived, pair_sem.at[0, k], pair_sem.at[1, k], (z * 2 + (1 - x), g)
        ).wait_recv()
        sums[...] = (own[x].astype(F32) + arrived[...].astype(F32)).astype(BF16)
        for step in range(1, n_z):
            to = lax.rem(z + step, n_z)
            send(
                remote(
                    sums.at[to],
                    landing.at[step - 1],
                    ring_sem.at[0, k, step],
                    ring_sem.at[1, k, step],
                    (to * 2 + x, g),
                )
            )

    def ring_end(k, sums, landing):
        result = sums[z].astype(F32)
        for step in range(1, n_z):
            source = lax.rem(z + n_z - step, n_z)
            remote(
                sums.at[z],
                landing.at[step - 1],
                ring_sem.at[0, k, step],
                ring_sem.at[1, k, step],
                (source * 2 + x, g),
            ).wait_recv()
            result = result + landing[step - 1].astype(F32)
        return result.astype(BF16)

    own[6].wait()
    own[7].wait()
    stores = []

    def expert_weight_grad(s):
        expert_grad[s] = lax.dot_general(
            saved[s], rows[s], (((0,), (0,)), ((), ())), preferred_element_type=F32
        ).astype(BF16)
        stores.append(pltpu.make_async_copy(expert_grad.at[s], expert_grad_hbm.at[s], out_sem.at[s]))
        stores[-1].start()

    for k in range(CHUNKS):
        if k < local:
            expert_weight_grad(k)
        ring_start(k, part.at[k], part_in.at[k], pair_sum.at[k], ring_in.at[k])
        if k == 1:
            for j in range(1, n_ex):
                source = lax.rem(g + n_ex - j, n_ex)
                remote(
                    hidden_piece(source),
                    hiddens.at[source],
                    hidden_sem.at[0, j],
                    hidden_sem.at[1, j],
                    (d, source),
                ).wait_recv()
            weight_grad_ref[...] = lax.dot_general(
                hiddens[...].reshape(tokens, unit),
                all_tokens,
                (((0,), (0,)), ((), ())),
                preferred_element_type=F32,
            ).astype(BF16)
    for s in range(CHUNKS, local):
        expert_weight_grad(s)
    ring_start(CHUNKS, spart, spart_in, spair_sum, sring_in)

    for k in range(CHUNKS):
        total[k] = ring_end(k, pair_sum.at[k], ring_in.at[k])
        gathered[k, g] = total[k]
        for j in range(1, n_ex):
            send(
                remote(
                    total.at[k],
                    gathered.at[k, g],
                    spread_sem.at[0, k, j],
                    spread_sem.at[1, k, j],
                    (d, lax.rem(g + j, n_ex)),
                )
            )
    hidden_grad_ref[...] = ring_end(CHUNKS, spair_sum, sring_in)

    high = lax.broadcasted_iota(jnp.int32, (piece, local * piece), 0)
    wide = lax.broadcasted_iota(jnp.int32, (piece, local * piece), 1)
    for k in range(CHUNKS):
        for j in range(1, n_ex):
            source = lax.rem(g + n_ex - j, n_ex)
            remote(
                total.at[k],
                gathered.at[k, source],
                spread_sem.at[0, k, j],
                spread_sem.at[1, k, j],
                (d, source),
            ).wait_recv()
        for s in range(local):
            wanted = new_ref[g * local + s]
            found = jnp.zeros((piece, width), F32)
            for p in range(n_ex):
                choice = jnp.zeros((piece, local * piece), F32)
                for q in range(local):
                    same = jnp.where(old_ref[p * local + q] == wanted, 1.0, 0.0)
                    choice = jnp.where(wide == high + q * piece, same, choice)
                found = found + jnp.dot(
                    choice.astype(BF16), gathered[k, p], preferred_element_type=F32
                )
            routed_ref[s, :, k * width : (k + 1) * width] = found.astype(BF16)

    for copy in stores:
        copy.wait()
    for copy in sent:
        copy.wait_send()


def on_device(
    n_dp,
    n_ex,
    grad_output,
    gate_probs,
    routing,
    old_weights,
    old_slot_expert,
    new_slot_expert,
    saved_hidden,
    shared_hidden,
    shared_weight,
):
    local, hidden, columns = old_weights.shape
    slot_rows = saved_hidden.shape[1]
    tok, chosen = routing.shape
    units_here = shared_weight.shape[0]
    units = shared_hidden.shape[1]
    sliced = units_here % 128 == 0
    if not sliced:
        shared_hidden = shared_hidden.reshape(tok, n_ex, units_here).transpose(1, 0, 2)
    piece = slot_rows // n_dp
    packed = local * piece
    width = hidden // CHUNKS
    share = units // n_dp
    n_z, n_y = n_dp // 2, n_ex // 2
    vmem = pl.BlockSpec(memory_space=pltpu.VMEM)
    anywhere = pl.BlockSpec(memory_space=pl.ANY)
    sem = pltpu.SemaphoreType.DMA
    expert_weight_grad, routed, hidden_grad, weight_grad = pl.pallas_call(
        functools.partial(exchange_kernel, n_dp, n_ex, sliced),
        out_shape=(
            jax.ShapeDtypeStruct((local, hidden, columns), BF16),
            jax.ShapeDtypeStruct((local, piece, hidden), BF16),
            jax.ShapeDtypeStruct((tok, share), BF16),
            jax.ShapeDtypeStruct((units_here, columns), BF16),
        ),
        in_specs=[anywhere] * 9,
        out_specs=(anywhere, vmem, vmem, vmem),
        scratch_shapes=[
            pltpu.SMEM(old_slot_expert.shape, jnp.int32),
            pltpu.SMEM(new_slot_expert.shape, jnp.int32),
            pltpu.VMEM((local, hidden, columns), BF16),
            pltpu.VMEM(saved_hidden.shape, BF16),
            pltpu.VMEM((local, hidden, columns), BF16),
            pltpu.VMEM((local, slot_rows, columns), BF16),
            pltpu.VMEM((n_ex, tok, columns), BF16),
            pltpu.VMEM((n_ex, chosen, tok), jnp.int32),
            pltpu.VMEM((n_ex, chosen, tok), F32),
            pltpu.VMEM((n_ex, tok, units_here), BF16),
            pltpu.VMEM((n_ex, units_here, columns), BF16),
            pltpu.VMEM((local, slot_rows, columns), BF16),
            pltpu.VMEM((slot_rows, width), F32),
            pltpu.VMEM((n_dp, packed, width), F32),
            pltpu.VMEM((CHUNKS, 2, n_z, packed, width), BF16),
            pltpu.VMEM((CHUNKS, n_z, packed, width), BF16),
            pltpu.VMEM((CHUNKS, n_z, packed, width), BF16),
            pltpu.VMEM((CHUNKS, n_z - 1, packed, width), BF16),
            pltpu.VMEM((CHUNKS, packed, width), BF16),
            pltpu.VMEM((CHUNKS, n_ex, packed, width), BF16),
            pltpu.VMEM((2, n_z, tok, share), BF16),
            pltpu.VMEM((n_z, tok, share), BF16),
            pltpu.VMEM((n_z, tok, share), BF16),
            pltpu.VMEM((n_z - 1, tok, share), BF16),
            sem((CHUNKS,)),
            sem((8,)),
            sem((local,)),
            sem((2, n_ex)),
            sem((2, n_ex)),
            sem((2, n_y)),
            sem((2, n_y)),
            sem((2, n_y)),
            sem((2, n_y)),
            sem((2, n_ex)),
            sem((2, CHUNKS + 1)),
            sem((2, CHUNKS + 1, n_z)),
            sem((2, CHUNKS, n_ex)),
        ],
        compiler_params=pltpu.CompilerParams(
            collective_id=0, has_side_effects=True, vmem_limit_bytes=60 * 1024 * 1024
        ),
    )(
        grad_output,
        routing.T,
        gate_probs.T,
        old_slot_expert,
        new_slot_expert,
        shared_hidden,
        shared_weight,
        old_weights,
        saved_hidden,
    )
    return expert_weight_grad, routed, hidden_grad, weight_grad


def solution(mesh):
    return jax.shard_map(
        functools.partial(on_device, mesh.shape["dp"], mesh.shape["expert"]),
        mesh=mesh,
        in_specs=(
            P("expert", "dp"),
            P("expert", None),
            P("expert", None),
            P("expert", None, "dp"),
            P(),
            P(),
            P("expert", None, None),
            P("expert", None),
            P("expert", "dp"),
        ),
        out_specs=(
            P("expert", None, "dp"),
            P("expert", "dp", None),
            P("expert", "dp"),
            P("expert", "dp"),
        ),
        check_vma=False,
    )
```

```python
import functools

import jax
import jax.numpy as jnp
from jax import lax
from jax.experimental import pallas as pl
from jax.experimental.pallas import tpu as pltpu
from jax.sharding import PartitionSpec as P

MESH = pl.DeviceIdType.MESH
F32 = jnp.float32
BF16 = jnp.bfloat16
CHUNKS = 2


def remote(src, dst, send, recv, device):
    return pltpu.make_async_remote_copy(
        src_ref=src, dst_ref=dst, send_sem=send, recv_sem=recv, device_id=device, device_id_type=MESH
    )


def exchange_kernel(
    n_dp,
    n_ex,
    sliced,
    grad_ref,
    route_ref,
    gate_ref,
    old_hbm,
    new_hbm,
    hidden_ref,
    shared_ref,
    weights_hbm,
    saved_hbm,
    expert_grad_hbm,
    routed_ref,
    hidden_grad_ref,
    weight_grad_ref,
    old_ref,
    new_ref,
    weights,
    saved,
    expert_grad,
    rows,
    grads,
    routes,
    gate_tables,
    hiddens,
    shareds,
    picked,
    product,
    stage,
    part,
    part_in,
    pair_sum,
    near_in,
    near_sum,
    far_in,
    total,
    gathered,
    spart,
    spart_in,
    spair_sum,
    sring_in,
    local_sem,
    own_sem,
    out_sem,
    route_sem,
    gate_sem,
    grad_sem,
    grad_pair_sem,
    shared_sem,
    shared_pair_sem,
    hidden_sem,
    pair_sem,
    near_sem,
    far_sem,
    ring_sem,
    spread_sem,
):
    d, g = lax.axis_index("dp"), lax.axis_index("expert")
    n_z, n_y = n_dp // 2, n_ex // 2
    z, x = d // 2, lax.rem(d, 2)
    y, c = g // 2, lax.rem(g, 2)
    local, slot_rows, columns = rows.shape
    cap = slot_rows // n_ex
    tok = grad_ref.shape[0]
    tokens = tok * n_ex
    chosen = route_ref.shape[0]
    piece = slot_rows // n_dp
    near, steps = part.shape[2], part.shape[3]
    part_rows = slot_rows // n_y
    units_sent = n_y * CHUNKS
    hidden = weights.shape[1]
    width = hidden // CHUNKS

    def pair_of(first):
        return (d, first * 2 + (1 - c))

    def line_dest(dy):
        return lax.rem(y + dy, n_y) * 2 + c

    def line_source(dy):
        return lax.rem(y + n_y - dy, n_y) * 2 + c

    unit = hiddens.shape[2]

    def hidden_piece(owner):
        if sliced:
            return hidden_ref.at[:, pl.ds(pl.multiple_of(owner * unit, unit), unit)]
        return hidden_ref.at[owner]

    own = [
        (old_hbm, old_ref),
        (new_hbm, new_ref),
        (route_ref, routes.at[g]),
        (gate_ref, gate_tables.at[g]),
        (grad_ref, grads.at[g]),
        (shared_ref, shareds.at[g]),
        (hidden_piece(g), hiddens.at[g]),
        (saved_hbm, saved),
    ]
    own = [pltpu.make_async_copy(a, b, own_sem.at[i]) for i, (a, b) in enumerate(own)]
    for copy in own:
        copy.start()
    loads = []
    for k in range(CHUNKS):
        cut = pl.ds(k * width, width)
        loads.append(
            pltpu.make_async_copy(weights_hbm.at[:, cut], weights.at[:, cut], local_sem.at[k])
        )
        loads[-1].start()

    barrier = pltpu.get_barrier_semaphore()
    peers = [(d, lax.rem(g + k, n_ex)) for k in range(1, n_ex)]
    peers += [(z * 2 + (1 - x), g)]
    peers += [(lax.rem(z + k, n_z) * 2 + x, g) for k in range(1, n_z)]
    for peer in peers:
        pl.semaphore_signal(barrier, inc=1, device_id=peer, device_id_type=MESH)
    pl.semaphore_wait(barrier, len(peers))

    sent = []

    def send(copy):
        copy.start()
        sent.append(copy)

    def gather_start(ref, buffer, sem, pair):
        for k in range(1, n_y):
            send(remote(ref, buffer.at[g], sem.at[0, k], sem.at[1, k], (d, line_dest(k))))
        send(remote(ref, buffer.at[g], pair.at[0, 0], pair.at[1, 0], (d, y * 2 + (1 - c))))

    def gather_forward(ref, buffer, sem, pair):
        for k in range(1, n_y):
            source = line_source(k)
            remote(ref, buffer.at[source], sem.at[0, k], sem.at[1, k], (d, source)).wait_recv()
            block = buffer.at[source]
            send(remote(block, block, pair.at[0, k], pair.at[1, k], (d, y * 2 + (1 - c))))

    def gather_end(ref, buffer, sem, pair, which=None):
        for k in which or range(n_y):
            source = lax.rem(y + n_y - k, n_y) * 2 + (1 - c)
            remote(ref, buffer.at[source], pair.at[0, k], pair.at[1, k], (d, source)).wait_recv()

    for k in range(1, n_ex):
        peer = lax.rem(g + k, n_ex)
        send(remote(route_ref, routes.at[g], route_sem.at[0, k], route_sem.at[1, k], (d, peer)))
        send(remote(gate_ref, gate_tables.at[g], gate_sem.at[0, k], gate_sem.at[1, k], (d, peer)))
    gather_start(grad_ref, grads, grad_sem, grad_pair_sem)

    for k in range(1, n_ex):
        source = lax.rem(g + n_ex - k, n_ex)
        remote(
            route_ref, routes.at[source], route_sem.at[0, k], route_sem.at[1, k], (d, source)
        ).wait_recv()
        remote(
            gate_ref, gate_tables.at[source], gate_sem.at[0, k], gate_sem.at[1, k], (d, source)
        ).wait_recv()
    for copy in own[:4]:
        copy.wait()
    place = lax.broadcasted_iota(jnp.int32, (2 * local, 1), 0)
    labels = jnp.zeros((2 * local, 1), F32)
    for s in range(local):
        labels = jnp.where(place == s, old_ref[g * local + s].astype(F32), labels)
        labels = jnp.where(place == local + s, new_ref[g * local + s].astype(F32), labels)
    before = (
        lax.broadcasted_iota(jnp.int32, (tok, tok), 0)
        < lax.broadcasted_iota(jnp.int32, (tok, tok), 1)
    ).astype(BF16)

    def codes_of(p, first):
        table, gate_table = routes[p].astype(F32), gate_tables[p]
        named = jnp.zeros((2 * local, tok), F32)
        gate = jnp.zeros((2 * local, tok), F32)
        for k in range(chosen):
            hit = table[k : k + 1, :] == labels
            named = jnp.where(hit, 1.0, named)
            gate = jnp.where(hit, gate_table[k : k + 1, :], gate)
        rank = jnp.dot(named.astype(BF16), before, preferred_element_type=F32)
        return jnp.where(named > 0, rank + float(first), -1.0), gate

    def joined(groups):
        pairs = [codes_of(p, i * cap) for i, p in enumerate(groups)]
        return [jnp.concatenate(parts, axis=1) for parts in zip(*pairs)]

    def build(s, codes, tokens_in, height):
        code, gate = codes
        row = lax.broadcasted_iota(jnp.int32, (height, code.shape[1]), 0).astype(F32)
        hit = code[s : s + 1, :] == row
        scale = jnp.sum(jnp.where(hit, gate[s : s + 1, :], 0.0), axis=1, keepdims=True)
        chosen_rows = jnp.dot(hit.astype(BF16), tokens_in, preferred_element_type=F32)
        return (chosen_rows * scale).astype(BF16)

    def pair_send(k, source, target):
        send(
            remote(
                source.at[1 - x], target, pair_sem.at[0, k], pair_sem.at[1, k], (z * 2 + (1 - x), g)
            )
        )

    zp, line = lax.rem(z, near), z // near
    n_line = n_z // near

    def near_start(u):
        remote(
            part.at[u, x], part_in.at[u], pair_sem.at[0, u], pair_sem.at[1, u], (z * 2 + (1 - x), g)
        ).wait_recv()
        pair_sum[u] = (part[u, x].astype(F32) + part_in[u].astype(F32)).astype(BF16)
        if near == 2:
            send(
                remote(
                    pair_sum.at[u, 1 - zp],
                    near_in.at[u],
                    near_sem.at[0, u],
                    near_sem.at[1, u],
                    ((line * 2 + (1 - zp)) * 2 + x, g),
                )
            )

    def finished_line(u, i):
        return lax.rem(y + n_y - u // CHUNKS, n_y) * steps + i

    def far_copy(u, i):
        to = finished_line(u, i)
        apart = lax.rem(to + n_line - line, n_line)
        return remote(
            near_sum.at[u, 0, i],
            far_in.at[u % CHUNKS, apart - 1],
            far_sem.at[0, u, i],
            far_sem.at[1, u % CHUNKS, apart],
            ((to * near + zp) * 2 + x, g),
        )

    def far_start(u):
        if near == 2:
            remote(
                pair_sum.at[u, zp],
                near_in.at[u],
                near_sem.at[0, u],
                near_sem.at[1, u],
                ((line * 2 + (1 - zp)) * 2 + x, g),
            ).wait_recv()
            near_sum[u, 0] = (pair_sum[u, zp].astype(F32) + near_in[u].astype(F32)).astype(BF16)
        else:
            near_sum[u, 0] = pair_sum[u, 0]
        for i in range(steps):

            @pl.when(finished_line(u, i) != line)
            def _():
                far_copy(u, i).start()

    def spread_copy(k, j):
        return remote(
            total.at[k],
            gathered.at[k, g],
            spread_sem.at[0, k, j],
            spread_sem.at[1, k, j],
            (d, lax.rem(g + j, n_ex)),
        )

    def finish(u):
        k = u % CHUNKS
        for i in range(steps):

            @pl.when(finished_line(u, i) == line)
            def _():
                result = near_sum[u, 0, i].astype(F32)
                for apart in range(1, n_line):
                    source = lax.rem(line + n_line - apart, n_line)
                    remote(
                        near_sum.at[u, 0, i],
                        far_in.at[k, apart - 1],
                        far_sem.at[0, u, i],
                        far_sem.at[1, k, apart],
                        ((source * near + zp) * 2 + x, g),
                    ).wait_recv()
                    result = result + far_in[k, apart - 1].astype(F32)
                total[k] = result.astype(BF16)
                gathered[k, g] = total[k]
                for j in range(1, n_ex):
                    spread_copy(k, j).start()

    def multiply(o):
        first = lax.rem(y + n_y - o, n_y) * 2
        codes = joined([first, first + 1])
        tokens_in = grads[pl.ds(first, 2)].reshape(2 * tok, columns)
        for s in range(local):
            picked[s] = build(s, codes, tokens_in, part_rows)
        for k in range(CHUNKS):
            u = o * CHUNKS + k
            if o == 0:
                loads[k].wait()
            for s in range(local):
                product[...] = lax.dot_general(
                    picked[s],
                    weights[s, k * width : (k + 1) * width, :],
                    (((1,), (1,)), ((), ())),
                    preferred_element_type=F32,
                )
                for t in range(n_dp // n_y):
                    stage[t, s * piece : (s + 1) * piece, :] = product[t * piece : (t + 1) * piece, :]
            for t in range(n_dp // n_y):
                part[u, t % 2, t // 2 % near, t // 2 // near] = stage[t].astype(BF16)
            pair_send(u, part.at[u], part_in.at[u])
            if u >= CHUNKS:
                near_start(u - CHUNKS)

    own[4].wait()
    gather_end(grad_ref, grads, grad_sem, grad_pair_sem, range(1))
    multiply(0)
    gather_forward(grad_ref, grads, grad_sem, grad_pair_sem)
    gather_start(shared_ref, shareds, shared_sem, shared_pair_sem)
    for k in range(1, n_ex):
        peer = lax.rem(g + k, n_ex)
        send(
            remote(
                hidden_piece(peer), hiddens.at[g], hidden_sem.at[0, k], hidden_sem.at[1, k], (d, peer)
            )
        )
    for o in range(1, n_y):
        gather_end(grad_ref, grads, grad_sem, grad_pair_sem, range(o, o + 1))
        multiply(o)
    all_tokens = grads[...].reshape(tokens, columns)
    all_codes = joined(range(n_ex))

    gather_forward(shared_ref, shareds, shared_sem, shared_pair_sem)
    for s in range(local):
        rows[s] = build(local + s, all_codes, all_tokens, slot_rows)
    gather_end(shared_ref, shareds, shared_sem, shared_pair_sem)
    own[5].wait()
    units = shared_ref.shape[0] * n_ex
    shared_all = shareds[...].reshape(units, columns)
    share = units // n_dp
    own_tokens = grads[g]
    for t in range(n_dp):
        spart[t % 2, t // 2] = lax.dot_general(
            own_tokens,
            shared_all[t * share : (t + 1) * share, :],
            (((1,), (1,)), ((), ())),
            preferred_element_type=F32,
        ).astype(BF16)
    pair_send(units_sent, spart, spart_in)

    def ring_start(k, own, arrived, sums, landing):
        remote(
            own.at[x], arrived, pair_sem.at[0, k], pair_sem.at[1, k], (z * 2 + (1 - x), g)
        ).wait_recv()
        sums[...] = (own[x].astype(F32) + arrived[...].astype(F32)).astype(BF16)
        for step in range(1, n_z):
            to = lax.rem(z + step, n_z)
            send(
                remote(
                    sums.at[to],
                    landing.at[step - 1],
                    ring_sem.at[0, step],
                    ring_sem.at[1, step],
                    (to * 2 + x, g),
                )
            )

    def ring_end(sums, landing):
        result = sums[z].astype(F32)
        for step in range(1, n_z):
            source = lax.rem(z + n_z - step, n_z)
            remote(
                sums.at[z],
                landing.at[step - 1],
                ring_sem.at[0, step],
                ring_sem.at[1, step],
                (source * 2 + x, g),
            ).wait_recv()
            result = result + landing[step - 1].astype(F32)
        return result.astype(BF16)

    own[6].wait()
    own[7].wait()
    stores = []

    def expert_weight_grad(s):
        expert_grad[s] = lax.dot_general(
            saved[s], rows[s], (((0,), (0,)), ((), ())), preferred_element_type=F32
        ).astype(BF16)
        stores.append(pltpu.make_async_copy(expert_grad.at[s], expert_grad_hbm.at[s], out_sem.at[s]))
        stores[-1].start()

    early, late = range(units_sent - CHUNKS), range(units_sent - CHUNKS, units_sent)
    for u in early:
        far_start(u)
    expert_weight_grad(0)
    for u in late:
        near_start(u)
    for s in range(1, local // 2):
        expert_weight_grad(s)
    for u in early:
        finish(u)
    for u in late:
        far_start(u)
    for s in range(max(1, local // 2), local):
        expert_weight_grad(s)
    ring_start(units_sent, spart, spart_in, spair_sum, sring_in)
    for u in late:
        finish(u)
    for j in range(1, n_ex):
        source = lax.rem(g + n_ex - j, n_ex)
        remote(
            hidden_piece(source),
            hiddens.at[source],
            hidden_sem.at[0, j],
            hidden_sem.at[1, j],
            (d, source),
        ).wait_recv()
    weight_grad_ref[...] = lax.dot_general(
        hiddens[...].reshape(tokens, unit),
        all_tokens,
        (((0,), (0,)), ((), ())),
        preferred_element_type=F32,
    ).astype(BF16)
    hidden_grad_ref[...] = ring_end(spair_sum, sring_in)

    high = lax.broadcasted_iota(jnp.int32, (piece, local * piece), 0)
    wide = lax.broadcasted_iota(jnp.int32, (piece, local * piece), 1)
    for k in range(CHUNKS):
        for j in range(1, n_ex):
            source = lax.rem(g + n_ex - j, n_ex)
            remote(
                total.at[k],
                gathered.at[k, source],
                spread_sem.at[0, k, j],
                spread_sem.at[1, k, j],
                (d, source),
            ).wait_recv()
        for s in range(local):
            wanted = new_ref[g * local + s]
            found = jnp.zeros((piece, width), F32)
            for p in range(n_ex):
                choice = jnp.zeros((piece, local * piece), F32)
                for q in range(local):
                    same = jnp.where(old_ref[p * local + q] == wanted, 1.0, 0.0)
                    choice = jnp.where(wide == high + q * piece, same, choice)
                found = found + jnp.dot(
                    choice.astype(BF16), gathered[k, p], preferred_element_type=F32
                )
            routed_ref[s, :, k * width : (k + 1) * width] = found.astype(BF16)

    for copy in stores:
        copy.wait()
    for copy in sent:
        copy.wait_send()
    for k in range(CHUNKS):
        for j in range(1, n_ex):
            spread_copy(k, j).wait_send()
    for u in range(units_sent):
        for i in range(steps):

            @pl.when(finished_line(u, i) != line)
            def _():
                far_copy(u, i).wait_send()


def on_device(
    n_dp,
    n_ex,
    grad_output,
    gate_probs,
    routing,
    old_weights,
    old_slot_expert,
    new_slot_expert,
    saved_hidden,
    shared_hidden,
    shared_weight,
):
    local, hidden, columns = old_weights.shape
    slot_rows = saved_hidden.shape[1]
    tok, chosen = routing.shape
    units_here = shared_weight.shape[0]
    units = shared_hidden.shape[1]
    sliced = units_here % 128 == 0
    if not sliced:
        shared_hidden = shared_hidden.reshape(tok, n_ex, units_here).transpose(1, 0, 2)
    piece = slot_rows // n_dp
    packed = local * piece
    width = hidden // CHUNKS
    share = units // n_dp
    n_z, n_y = n_dp // 2, n_ex // 2
    ends = n_dp // n_y // 2
    near = 2 if ends % 2 == 0 else 1
    steps = ends // near
    units_sent = n_y * CHUNKS
    vmem = pl.BlockSpec(memory_space=pltpu.VMEM)
    anywhere = pl.BlockSpec(memory_space=pl.ANY)
    sem = pltpu.SemaphoreType.DMA
    expert_weight_grad, routed, hidden_grad, weight_grad = pl.pallas_call(
        functools.partial(exchange_kernel, n_dp, n_ex, sliced),
        out_shape=(
            jax.ShapeDtypeStruct((local, hidden, columns), BF16),
            jax.ShapeDtypeStruct((local, piece, hidden), BF16),
            jax.ShapeDtypeStruct((tok, share), BF16),
            jax.ShapeDtypeStruct((units_here, columns), BF16),
        ),
        in_specs=[anywhere] * 9,
        out_specs=(anywhere, vmem, vmem, vmem),
        scratch_shapes=[
            pltpu.SMEM(old_slot_expert.shape, jnp.int32),
            pltpu.SMEM(new_slot_expert.shape, jnp.int32),
            pltpu.VMEM((local, hidden, columns), BF16),
            pltpu.VMEM(saved_hidden.shape, BF16),
            pltpu.VMEM((local, hidden, columns), BF16),
            pltpu.VMEM((local, slot_rows, columns), BF16),
            pltpu.VMEM((n_ex, tok, columns), BF16),
            pltpu.VMEM((n_ex, chosen, tok), jnp.int32),
            pltpu.VMEM((n_ex, chosen, tok), F32),
            pltpu.VMEM((n_ex, tok, units_here), BF16),
            pltpu.VMEM((n_ex, units_here, columns), BF16),
            pltpu.VMEM((local, slot_rows // n_y, columns), BF16),
            pltpu.VMEM((slot_rows // n_y, width), F32),
            pltpu.VMEM((n_dp // n_y, packed, width), F32),
            pltpu.VMEM((units_sent, 2, near, steps, packed, width), BF16),
            pltpu.VMEM((units_sent, near, steps, packed, width), BF16),
            pltpu.VMEM((units_sent, near, steps, packed, width), BF16),
            pltpu.VMEM((units_sent, steps, packed, width), BF16),
            pltpu.VMEM((units_sent, 1, steps, packed, width), BF16),
            pltpu.VMEM((CHUNKS, n_z // near - 1, packed, width), BF16),
            pltpu.VMEM((CHUNKS, packed, width), BF16),
            pltpu.VMEM((CHUNKS, n_ex, packed, width), BF16),
            pltpu.VMEM((2, n_z, tok, share), BF16),
            pltpu.VMEM((n_z, tok, share), BF16),
            pltpu.VMEM((n_z, tok, share), BF16),
            pltpu.VMEM((n_z - 1, tok, share), BF16),
            sem((CHUNKS,)),
            sem((8,)),
            sem((local,)),
            sem((2, n_ex)),
            sem((2, n_ex)),
            sem((2, n_y)),
            sem((2, n_y)),
            sem((2, n_y)),
            sem((2, n_y)),
            sem((2, n_ex)),
            sem((2, units_sent + 1)),
            sem((2, units_sent)),
            sem((2, units_sent, max(steps, n_z // near))),
            sem((2, n_z)),
            sem((2, CHUNKS, n_ex)),
        ],
        compiler_params=pltpu.CompilerParams(
            collective_id=0, has_side_effects=True, vmem_limit_bytes=60 * 1024 * 1024
        ),
    )(
        grad_output,
        routing.T,
        gate_probs.T,
        old_slot_expert,
        new_slot_expert,
        shared_hidden,
        shared_weight,
        old_weights,
        saved_hidden,
    )
    return expert_weight_grad, routed, hidden_grad, weight_grad


def solution(mesh):
    return jax.shard_map(
        functools.partial(on_device, mesh.shape["dp"], mesh.shape["expert"]),
        mesh=mesh,
        in_specs=(
            P("expert", "dp"),
            P("expert", None),
            P("expert", None),
            P("expert", None, "dp"),
            P(),
            P(),
            P("expert", None, None),
            P("expert", None),
            P("expert", "dp"),
        ),
        out_specs=(
            P("expert", None, "dp"),
            P("expert", "dp", None),
            P("expert", "dp"),
            P("expert", "dp"),
        ),
        check_vma=False,
    )
```

```python
import functools

import jax
import jax.numpy as jnp
from jax import lax
from jax.experimental import pallas as pl
from jax.experimental.pallas import tpu as pltpu
from jax.sharding import PartitionSpec as P

MESH = pl.DeviceIdType.MESH
F32 = jnp.float32
BF16 = jnp.bfloat16
CHUNKS = 2


def remote(src, dst, send, recv, device):
    return pltpu.make_async_remote_copy(
        src_ref=src, dst_ref=dst, send_sem=send, recv_sem=recv, device_id=device, device_id_type=MESH
    )


def exchange_kernel(
    n_dp,
    n_ex,
    sliced,
    grad_ref,
    route_ref,
    gate_ref,
    old_hbm,
    new_hbm,
    hidden_ref,
    shared_ref,
    weights_hbm,
    saved_hbm,
    expert_grad_hbm,
    routed_ref,
    hidden_grad_ref,
    weight_grad_ref,
    old_ref,
    new_ref,
    weights,
    saved,
    expert_grad,
    rows,
    grads,
    routes,
    gate_tables,
    hiddens,
    shareds,
    picked,
    product,
    stage,
    part,
    part_in,
    pair_sum,
    near_in,
    near_sum,
    far_in,
    total,
    gathered,
    spart,
    spart_in,
    spair_sum,
    sring_in,
    local_sem,
    own_sem,
    out_sem,
    route_sem,
    gate_sem,
    grad_sem,
    grad_pair_sem,
    shared_sem,
    shared_pair_sem,
    hidden_sem,
    pair_sem,
    near_sem,
    far_sem,
    ring_sem,
    spread_sem,
):
    d, g = lax.axis_index("dp"), lax.axis_index("expert")
    n_z, n_y = n_dp // 2, n_ex // 2
    z, x = d // 2, lax.rem(d, 2)
    y, c = g // 2, lax.rem(g, 2)
    local, slot_rows, columns = rows.shape
    cap = slot_rows // n_ex
    tok = grad_ref.shape[0]
    tokens = tok * n_ex
    chosen = route_ref.shape[0]
    piece = slot_rows // n_dp
    near, steps = part.shape[2], part.shape[3]
    part_rows = slot_rows // n_y
    units_sent = n_y * CHUNKS
    hidden = weights.shape[1]
    width = hidden // CHUNKS

    def pair_of(first):
        return (d, first * 2 + (1 - c))

    def line_dest(dy):
        return lax.rem(y + dy, n_y) * 2 + c

    def line_source(dy):
        return lax.rem(y + n_y - dy, n_y) * 2 + c

    unit = hiddens.shape[2]

    def hidden_piece(owner):
        if sliced:
            return hidden_ref.at[:, pl.ds(pl.multiple_of(owner * unit, unit), unit)]
        return hidden_ref.at[owner]

    own = [
        (old_hbm, old_ref),
        (new_hbm, new_ref),
        (route_ref, routes.at[g]),
        (gate_ref, gate_tables.at[g]),
        (grad_ref, grads.at[g]),
        (shared_ref, shareds.at[g]),
        (hidden_piece(g), hiddens.at[g]),
        (saved_hbm, saved),
    ]
    own = [pltpu.make_async_copy(a, b, own_sem.at[i]) for i, (a, b) in enumerate(own)]
    for copy in own:
        copy.start()
    loads = []
    for k in range(CHUNKS):
        cut = pl.ds(k * width, width)
        loads.append(
            pltpu.make_async_copy(weights_hbm.at[:, cut], weights.at[:, cut], local_sem.at[k])
        )
        loads[-1].start()

    barrier = pltpu.get_barrier_semaphore()
    peers = [(d, lax.rem(g + k, n_ex)) for k in range(1, n_ex)]
    peers += [(z * 2 + (1 - x), g)]
    peers += [(lax.rem(z + k, n_z) * 2 + x, g) for k in range(1, n_z)]
    for peer in peers:
        pl.semaphore_signal(barrier, inc=1, device_id=peer, device_id_type=MESH)
    pl.semaphore_wait(barrier, len(peers))

    sent = []

    def send(copy):
        copy.start()
        sent.append(copy)

    def gather_start(ref, buffer, sem, pair):
        for k in range(1, n_y):
            send(remote(ref, buffer.at[g], sem.at[0, k], sem.at[1, k], (d, line_dest(k))))
        send(remote(ref, buffer.at[g], pair.at[0, 0], pair.at[1, 0], (d, y * 2 + (1 - c))))

    def gather_forward(ref, buffer, sem, pair):
        for k in range(1, n_y):
            source = line_source(k)
            remote(ref, buffer.at[source], sem.at[0, k], sem.at[1, k], (d, source)).wait_recv()
            block = buffer.at[source]
            send(remote(block, block, pair.at[0, k], pair.at[1, k], (d, y * 2 + (1 - c))))

    def gather_end(ref, buffer, sem, pair, which=None):
        for k in which or range(n_y):
            source = lax.rem(y + n_y - k, n_y) * 2 + (1 - c)
            remote(ref, buffer.at[source], pair.at[0, k], pair.at[1, k], (d, source)).wait_recv()

    for k in range(1, n_ex):
        peer = lax.rem(g + k, n_ex)
        send(remote(route_ref, routes.at[g], route_sem.at[0, k], route_sem.at[1, k], (d, peer)))
        send(remote(gate_ref, gate_tables.at[g], gate_sem.at[0, k], gate_sem.at[1, k], (d, peer)))
    gather_start(grad_ref, grads, grad_sem, grad_pair_sem)

    for k in range(1, n_ex):
        source = lax.rem(g + n_ex - k, n_ex)
        remote(
            route_ref, routes.at[source], route_sem.at[0, k], route_sem.at[1, k], (d, source)
        ).wait_recv()
        remote(
            gate_ref, gate_tables.at[source], gate_sem.at[0, k], gate_sem.at[1, k], (d, source)
        ).wait_recv()
    for copy in own[:4]:
        copy.wait()
    place = lax.broadcasted_iota(jnp.int32, (2 * local, 1), 0)
    labels = jnp.zeros((2 * local, 1), F32)
    for s in range(local):
        labels = jnp.where(place == s, old_ref[g * local + s].astype(F32), labels)
        labels = jnp.where(place == local + s, new_ref[g * local + s].astype(F32), labels)
    before = (
        lax.broadcasted_iota(jnp.int32, (tok, tok), 0)
        < lax.broadcasted_iota(jnp.int32, (tok, tok), 1)
    ).astype(BF16)

    def codes_of(p, first):
        table, gate_table = routes[p].astype(F32), gate_tables[p]
        named = jnp.zeros((2 * local, tok), F32)
        gate = jnp.zeros((2 * local, tok), F32)
        for k in range(chosen):
            hit = table[k : k + 1, :] == labels
            named = jnp.where(hit, 1.0, named)
            gate = jnp.where(hit, gate_table[k : k + 1, :], gate)
        rank = jnp.dot(named.astype(BF16), before, preferred_element_type=F32)
        return jnp.where(named > 0, rank + float(first), -1.0), gate

    def joined(groups):
        pairs = [codes_of(p, i * cap) for i, p in enumerate(groups)]
        return [jnp.concatenate(parts, axis=1) for parts in zip(*pairs)]

    def build(s, codes, tokens_in, height):
        code, gate = codes
        row = lax.broadcasted_iota(jnp.int32, (height, code.shape[1]), 0).astype(F32)
        hit = code[s : s + 1, :] == row
        scale = jnp.sum(jnp.where(hit, gate[s : s + 1, :], 0.0), axis=1, keepdims=True)
        chosen_rows = jnp.dot(hit.astype(BF16), tokens_in, preferred_element_type=F32)
        return (chosen_rows * scale).astype(BF16)

    def pair_send(k, source, target):
        send(
            remote(
                source.at[1 - x], target, pair_sem.at[0, k], pair_sem.at[1, k], (z * 2 + (1 - x), g)
            )
        )

    zp, line = lax.rem(z, near), z // near
    n_line = n_z // near

    def near_start(u):
        remote(
            part.at[u, x], part_in.at[u], pair_sem.at[0, u], pair_sem.at[1, u], (z * 2 + (1 - x), g)
        ).wait_recv()
        pair_sum[u] = (part[u, x].astype(F32) + part_in[u].astype(F32)).astype(BF16)
        if near == 2:
            send(
                remote(
                    pair_sum.at[u, 1 - zp],
                    near_in.at[u],
                    near_sem.at[0, u],
                    near_sem.at[1, u],
                    ((line * 2 + (1 - zp)) * 2 + x, g),
                )
            )

    def finished_line(u, i):
        return lax.rem(y + n_y - u // CHUNKS, n_y) * steps + i

    def far_copy(u, i):
        to = finished_line(u, i)
        apart = lax.rem(to + n_line - line, n_line)
        return remote(
            near_sum.at[u, 0, i],
            far_in.at[u % CHUNKS, apart - 1],
            far_sem.at[0, u, i],
            far_sem.at[1, u % CHUNKS, apart],
            ((to * near + zp) * 2 + x, g),
        )

    def far_start(u):
        if near == 2:
            remote(
                pair_sum.at[u, zp],
                near_in.at[u],
                near_sem.at[0, u],
                near_sem.at[1, u],
                ((line * 2 + (1 - zp)) * 2 + x, g),
            ).wait_recv()
            near_sum[u, 0] = (pair_sum[u, zp].astype(F32) + near_in[u].astype(F32)).astype(BF16)
        else:
            near_sum[u, 0] = pair_sum[u, 0]
        for i in range(steps):

            @pl.when(finished_line(u, i) != line)
            def _():
                far_copy(u, i).start()

    def spread_copy(k, j):
        return remote(
            total.at[k],
            gathered.at[k, g],
            spread_sem.at[0, k, j],
            spread_sem.at[1, k, j],
            (d, lax.rem(g + j, n_ex)),
        )

    def finish(u):
        k = u % CHUNKS
        for i in range(steps):

            @pl.when(finished_line(u, i) == line)
            def _():
                result = near_sum[u, 0, i].astype(F32)
                for apart in range(1, n_line):
                    source = lax.rem(line + n_line - apart, n_line)
                    remote(
                        near_sum.at[u, 0, i],
                        far_in.at[k, apart - 1],
                        far_sem.at[0, u, i],
                        far_sem.at[1, k, apart],
                        ((source * near + zp) * 2 + x, g),
                    ).wait_recv()
                    result = result + far_in[k, apart - 1].astype(F32)
                total[k] = result.astype(BF16)
                gathered[k, g] = total[k]
                for j in range(1, n_ex):
                    spread_copy(k, j).start()

    def multiply(o):
        first = lax.rem(y + n_y - o, n_y) * 2
        codes = joined([first, first + 1])
        tokens_in = grads[pl.ds(first, 2)].reshape(2 * tok, columns)
        for s in range(local):
            picked[s] = build(s, codes, tokens_in, part_rows)
        for k in range(CHUNKS):
            u = o * CHUNKS + k
            if o == 0:
                loads[k].wait()
            for s in range(local):
                product[...] = lax.dot_general(
                    picked[s],
                    weights[s, k * width : (k + 1) * width, :],
                    (((1,), (1,)), ((), ())),
                    preferred_element_type=F32,
                )
                for t in range(n_dp // n_y):
                    stage[t, s * piece : (s + 1) * piece, :] = product[t * piece : (t + 1) * piece, :]
            for t in range(n_dp // n_y):
                part[u, t % 2, t // 2 % near, t // 2 // near] = stage[t].astype(BF16)
            pair_send(u, part.at[u], part_in.at[u])
            if u >= CHUNKS:
                near_start(u - CHUNKS)

    own[4].wait()
    gather_end(grad_ref, grads, grad_sem, grad_pair_sem, range(1))
    multiply(0)
    gather_forward(grad_ref, grads, grad_sem, grad_pair_sem)
    gather_start(shared_ref, shareds, shared_sem, shared_pair_sem)
    for k in range(1, n_ex):
        peer = lax.rem(g + k, n_ex)
        send(
            remote(
                hidden_piece(peer), hiddens.at[g], hidden_sem.at[0, k], hidden_sem.at[1, k], (d, peer)
            )
        )
    for o in range(1, n_y):
        gather_end(grad_ref, grads, grad_sem, grad_pair_sem, range(o, o + 1))
        multiply(o)
    all_tokens = grads[...].reshape(tokens, columns)
    all_codes = joined(range(n_ex))

    gather_forward(shared_ref, shareds, shared_sem, shared_pair_sem)
    gather_end(shared_ref, shareds, shared_sem, shared_pair_sem)
    own[5].wait()
    units = shared_ref.shape[0] * n_ex
    shared_all = shareds[...].reshape(units, columns)
    share = units // n_dp
    own_tokens = grads[g]
    for t in range(n_dp):
        spart[t % 2, t // 2] = lax.dot_general(
            own_tokens,
            shared_all[t * share : (t + 1) * share, :],
            (((1,), (1,)), ((), ())),
            preferred_element_type=F32,
        ).astype(BF16)
    pair_send(units_sent, spart, spart_in)

    def ring_start(k, own, arrived, sums, landing):
        remote(
            own.at[x], arrived, pair_sem.at[0, k], pair_sem.at[1, k], (z * 2 + (1 - x), g)
        ).wait_recv()
        sums[...] = (own[x].astype(F32) + arrived[...].astype(F32)).astype(BF16)
        for step in range(1, n_z):
            to = lax.rem(z + step, n_z)
            send(
                remote(
                    sums.at[to],
                    landing.at[step - 1],
                    ring_sem.at[0, step],
                    ring_sem.at[1, step],
                    (to * 2 + x, g),
                )
            )

    def ring_end(sums, landing):
        result = sums[z].astype(F32)
        for step in range(1, n_z):
            source = lax.rem(z + n_z - step, n_z)
            remote(
                sums.at[z],
                landing.at[step - 1],
                ring_sem.at[0, step],
                ring_sem.at[1, step],
                (source * 2 + x, g),
            ).wait_recv()
            result = result + landing[step - 1].astype(F32)
        return result.astype(BF16)

    own[6].wait()
    own[7].wait()
    stores = []

    def expert_weight_grad(s):
        expert_grad[s] = lax.dot_general(
            saved[s], rows[s], (((0,), (0,)), ((), ())), preferred_element_type=F32
        ).astype(BF16)
        stores.append(pltpu.make_async_copy(expert_grad.at[s], expert_grad_hbm.at[s], out_sem.at[s]))
        stores[-1].start()

    early, late = range(units_sent - CHUNKS), range(units_sent - CHUNKS, units_sent)
    for u in early:
        far_start(u)
    for u in late:
        near_start(u)
    for s in range(local):
        rows[s] = build(local + s, all_codes, all_tokens, slot_rows)
    for u in early:
        finish(u)
    for u in late:
        far_start(u)
    ring_start(units_sent, spart, spart_in, spair_sum, sring_in)
    expert_weight_grad(0)
    for u in late:
        finish(u)
    for s in range(1, local):
        expert_weight_grad(s)
    for j in range(1, n_ex):
        source = lax.rem(g + n_ex - j, n_ex)
        remote(
            hidden_piece(source),
            hiddens.at[source],
            hidden_sem.at[0, j],
            hidden_sem.at[1, j],
            (d, source),
        ).wait_recv()
    weight_grad_ref[...] = lax.dot_general(
        hiddens[...].reshape(tokens, unit),
        all_tokens,
        (((0,), (0,)), ((), ())),
        preferred_element_type=F32,
    ).astype(BF16)
    hidden_grad_ref[...] = ring_end(spair_sum, sring_in)

    def labelled(shape, axis, listing, first):
        place = lax.broadcasted_iota(jnp.int32, shape, axis)
        label, offset = jnp.zeros(shape, jnp.int32), place
        for q in range(local):
            inside = place >= q * piece
            label = jnp.where(inside, listing[first + q], label)
            offset = jnp.where(inside, place - q * piece, offset)
        return label, offset

    packed = local * piece
    wanted, high = labelled((packed, packed), 0, new_ref, g * local)
    choices = []
    for p in range(n_ex):
        held, wide = labelled((packed, packed), 1, old_ref, p * local)
        choices.append(jnp.where((wanted == held) & (high == wide), 1.0, 0.0).astype(BF16))
    for k in range(CHUNKS):
        for j in range(1, n_ex):
            source = lax.rem(g + n_ex - j, n_ex)
            remote(
                total.at[k],
                gathered.at[k, source],
                spread_sem.at[0, k, j],
                spread_sem.at[1, k, j],
                (d, source),
            ).wait_recv()
        found = jnp.zeros((packed, width), F32)
        for p in range(n_ex):
            found = found + jnp.dot(choices[p], gathered[k, p], preferred_element_type=F32)
        routed_ref[:, k * width : (k + 1) * width] = found.astype(BF16)

    for copy in stores:
        copy.wait()
    for copy in sent:
        copy.wait_send()
    for k in range(CHUNKS):
        for j in range(1, n_ex):
            spread_copy(k, j).wait_send()
    for u in range(units_sent):
        for i in range(steps):

            @pl.when(finished_line(u, i) != line)
            def _():
                far_copy(u, i).wait_send()


def on_device(
    n_dp,
    n_ex,
    grad_output,
    gate_probs,
    routing,
    old_weights,
    old_slot_expert,
    new_slot_expert,
    saved_hidden,
    shared_hidden,
    shared_weight,
):
    local, hidden, columns = old_weights.shape
    slot_rows = saved_hidden.shape[1]
    tok, chosen = routing.shape
    units_here = shared_weight.shape[0]
    units = shared_hidden.shape[1]
    sliced = units_here % 128 == 0
    if not sliced:
        shared_hidden = shared_hidden.reshape(tok, n_ex, units_here).transpose(1, 0, 2)
    piece = slot_rows // n_dp
    packed = local * piece
    width = hidden // CHUNKS
    share = units // n_dp
    n_z, n_y = n_dp // 2, n_ex // 2
    ends = n_dp // n_y // 2
    near = 2 if ends % 2 == 0 else 1
    steps = ends // near
    units_sent = n_y * CHUNKS
    vmem = pl.BlockSpec(memory_space=pltpu.VMEM)
    anywhere = pl.BlockSpec(memory_space=pl.ANY)
    sem = pltpu.SemaphoreType.DMA
    expert_weight_grad, routed, hidden_grad, weight_grad = pl.pallas_call(
        functools.partial(exchange_kernel, n_dp, n_ex, sliced),
        out_shape=(
            jax.ShapeDtypeStruct((local, hidden, columns), BF16),
            jax.ShapeDtypeStruct((packed, hidden), BF16),
            jax.ShapeDtypeStruct((tok, share), BF16),
            jax.ShapeDtypeStruct((units_here, columns), BF16),
        ),
        in_specs=[anywhere] * 9,
        out_specs=(anywhere, vmem, vmem, vmem),
        scratch_shapes=[
            pltpu.SMEM(old_slot_expert.shape, jnp.int32),
            pltpu.SMEM(new_slot_expert.shape, jnp.int32),
            pltpu.VMEM((local, hidden, columns), BF16),
            pltpu.VMEM(saved_hidden.shape, BF16),
            pltpu.VMEM((local, hidden, columns), BF16),
            pltpu.VMEM((local, slot_rows, columns), BF16),
            pltpu.VMEM((n_ex, tok, columns), BF16),
            pltpu.VMEM((n_ex, chosen, tok), jnp.int32),
            pltpu.VMEM((n_ex, chosen, tok), F32),
            pltpu.VMEM((n_ex, tok, units_here), BF16),
            pltpu.VMEM((n_ex, units_here, columns), BF16),
            pltpu.VMEM((local, slot_rows // n_y, columns), BF16),
            pltpu.VMEM((slot_rows // n_y, width), F32),
            pltpu.VMEM((n_dp // n_y, packed, width), F32),
            pltpu.VMEM((units_sent, 2, near, steps, packed, width), BF16),
            pltpu.VMEM((units_sent, near, steps, packed, width), BF16),
            pltpu.VMEM((units_sent, near, steps, packed, width), BF16),
            pltpu.VMEM((units_sent, steps, packed, width), BF16),
            pltpu.VMEM((units_sent, 1, steps, packed, width), BF16),
            pltpu.VMEM((CHUNKS, n_z // near - 1, packed, width), BF16),
            pltpu.VMEM((CHUNKS, packed, width), BF16),
            pltpu.VMEM((CHUNKS, n_ex, packed, width), BF16),
            pltpu.VMEM((2, n_z, tok, share), BF16),
            pltpu.VMEM((n_z, tok, share), BF16),
            pltpu.VMEM((n_z, tok, share), BF16),
            pltpu.VMEM((n_z - 1, tok, share), BF16),
            sem((CHUNKS,)),
            sem((8,)),
            sem((local,)),
            sem((2, n_ex)),
            sem((2, n_ex)),
            sem((2, n_y)),
            sem((2, n_y)),
            sem((2, n_y)),
            sem((2, n_y)),
            sem((2, n_ex)),
            sem((2, units_sent + 1)),
            sem((2, units_sent)),
            sem((2, units_sent, max(steps, n_z // near))),
            sem((2, n_z)),
            sem((2, CHUNKS, n_ex)),
        ],
        compiler_params=pltpu.CompilerParams(
            collective_id=0, has_side_effects=True, vmem_limit_bytes=60 * 1024 * 1024
        ),
    )(
        grad_output,
        routing.T,
        gate_probs.T,
        old_slot_expert,
        new_slot_expert,
        shared_hidden,
        shared_weight,
        old_weights,
        saved_hidden,
    )
    routed = routed.reshape(local, piece, hidden)
    return expert_weight_grad, routed, hidden_grad, weight_grad


def solution(mesh):
    return jax.shard_map(
        functools.partial(on_device, mesh.shape["dp"], mesh.shape["expert"]),
        mesh=mesh,
        in_specs=(
            P("expert", "dp"),
            P("expert", None),
            P("expert", None),
            P("expert", None, "dp"),
            P(),
            P(),
            P("expert", None, None),
            P("expert", None),
            P("expert", "dp"),
        ),
        out_specs=(
            P("expert", None, "dp"),
            P("expert", "dp", None),
            P("expert", "dp"),
            P("expert", "dp"),
        ),
        check_vma=False,
    )
```

```python
import functools

import jax
import jax.numpy as jnp
from jax import lax
from jax.experimental import pallas as pl
from jax.experimental.pallas import tpu as pltpu
from jax.sharding import PartitionSpec as P

MESH = pl.DeviceIdType.MESH
F32 = jnp.float32
BF16 = jnp.bfloat16
CHUNKS = 2


def remote(src, dst, send, recv, device):
    return pltpu.make_async_remote_copy(
        src_ref=src, dst_ref=dst, send_sem=send, recv_sem=recv, device_id=device, device_id_type=MESH
    )


def exchange_kernel(
    n_dp,
    n_ex,
    sliced,
    grad_ref,
    route_ref,
    gate_ref,
    old_hbm,
    new_hbm,
    hidden_ref,
    shared_ref,
    weights_hbm,
    saved_hbm,
    expert_grad_hbm,
    routed_ref,
    hidden_grad_ref,
    weight_grad_ref,
    old_ref,
    new_ref,
    weights,
    saved,
    expert_grad,
    rows,
    grads,
    routes,
    gate_tables,
    hiddens,
    shareds,
    picked,
    product,
    stage,
    part,
    part_in,
    pair_sum,
    near_in,
    near_sum,
    far_in,
    total,
    gathered,
    spart,
    spart_in,
    spair_sum,
    sring_in,
    local_sem,
    own_sem,
    out_sem,
    route_sem,
    gate_sem,
    grad_sem,
    grad_pair_sem,
    shared_sem,
    shared_pair_sem,
    hidden_sem,
    pair_sem,
    near_sem,
    far_sem,
    ring_sem,
    spread_sem,
):
    d, g = lax.axis_index("dp"), lax.axis_index("expert")
    n_z, n_y = n_dp // 2, n_ex // 2
    z, x = d // 2, lax.rem(d, 2)
    y, c = g // 2, lax.rem(g, 2)
    local, slot_rows, columns = rows.shape
    cap = slot_rows // n_ex
    tok = grad_ref.shape[0]
    tokens = tok * n_ex
    chosen = route_ref.shape[0]
    piece = slot_rows // n_dp
    near, steps = part.shape[2], part.shape[3]
    part_rows = slot_rows // n_y
    units_sent = n_y * CHUNKS
    hidden = weights.shape[1]
    width = hidden // CHUNKS

    def pair_of(first):
        return (d, first * 2 + (1 - c))

    def line_dest(dy):
        return lax.rem(y + dy, n_y) * 2 + c

    def line_source(dy):
        return lax.rem(y + n_y - dy, n_y) * 2 + c

    unit = hiddens.shape[2]

    def hidden_piece(owner):
        if sliced:
            return hidden_ref.at[:, pl.ds(pl.multiple_of(owner * unit, unit), unit)]
        return hidden_ref.at[owner]

    own = [
        (old_hbm, old_ref),
        (new_hbm, new_ref),
        (route_ref, routes.at[g]),
        (gate_ref, gate_tables.at[g]),
        (grad_ref, grads.at[g]),
        (shared_ref, shareds.at[g]),
        (hidden_piece(g), hiddens.at[g]),
        (saved_hbm, saved),
    ]
    own = [pltpu.make_async_copy(a, b, own_sem.at[i]) for i, (a, b) in enumerate(own)]
    for copy in own:
        copy.start()
    loads = []
    for k in range(CHUNKS):
        cut = pl.ds(k * width, width)
        loads.append(
            pltpu.make_async_copy(weights_hbm.at[:, cut], weights.at[:, cut], local_sem.at[k])
        )
        loads[-1].start()

    barrier = pltpu.get_barrier_semaphore()
    peers = [(d, lax.rem(g + k, n_ex)) for k in range(1, n_ex)]
    peers += [(z * 2 + (1 - x), g)]
    peers += [(lax.rem(z + k, n_z) * 2 + x, g) for k in range(1, n_z)]
    for peer in peers:
        pl.semaphore_signal(barrier, inc=1, device_id=peer, device_id_type=MESH)
    pl.semaphore_wait(barrier, len(peers))

    sent = []

    def send(copy):
        copy.start()
        sent.append(copy)

    def gather_start(ref, buffer, sem, pair):
        for k in range(1, n_y):
            send(remote(ref, buffer.at[g], sem.at[0, k], sem.at[1, k], (d, line_dest(k))))
        send(remote(ref, buffer.at[g], pair.at[0, 0], pair.at[1, 0], (d, y * 2 + (1 - c))))

    def gather_forward(ref, buffer, sem, pair):
        for k in range(1, n_y):
            source = line_source(k)
            remote(ref, buffer.at[source], sem.at[0, k], sem.at[1, k], (d, source)).wait_recv()
            block = buffer.at[source]
            send(remote(block, block, pair.at[0, k], pair.at[1, k], (d, y * 2 + (1 - c))))

    def gather_end(ref, buffer, sem, pair, which=None):
        for k in which or range(n_y):
            source = lax.rem(y + n_y - k, n_y) * 2 + (1 - c)
            remote(ref, buffer.at[source], pair.at[0, k], pair.at[1, k], (d, source)).wait_recv()

    for k in range(1, n_ex):
        peer = lax.rem(g + k, n_ex)
        send(remote(route_ref, routes.at[g], route_sem.at[0, k], route_sem.at[1, k], (d, peer)))
        send(remote(gate_ref, gate_tables.at[g], gate_sem.at[0, k], gate_sem.at[1, k], (d, peer)))
    gather_start(grad_ref, grads, grad_sem, grad_pair_sem)

    for k in range(1, n_ex):
        source = lax.rem(g + n_ex - k, n_ex)
        remote(
            route_ref, routes.at[source], route_sem.at[0, k], route_sem.at[1, k], (d, source)
        ).wait_recv()
        remote(
            gate_ref, gate_tables.at[source], gate_sem.at[0, k], gate_sem.at[1, k], (d, source)
        ).wait_recv()
    for copy in own[:4]:
        copy.wait()
    place = lax.broadcasted_iota(jnp.int32, (2 * local, 1), 0)
    labels = jnp.zeros((2 * local, 1), F32)
    for s in range(local):
        labels = jnp.where(place == s, old_ref[g * local + s].astype(F32), labels)
        labels = jnp.where(place == local + s, new_ref[g * local + s].astype(F32), labels)
    before = (
        lax.broadcasted_iota(jnp.int32, (tok, tok), 0)
        < lax.broadcasted_iota(jnp.int32, (tok, tok), 1)
    ).astype(BF16)

    def codes_of(p, first):
        table, gate_table = routes[p].astype(F32), gate_tables[p]
        named = jnp.zeros((2 * local, tok), F32)
        gate = jnp.zeros((2 * local, tok), F32)
        for k in range(chosen):
            hit = table[k : k + 1, :] == labels
            named = jnp.where(hit, 1.0, named)
            gate = jnp.where(hit, gate_table[k : k + 1, :], gate)
        rank = jnp.dot(named.astype(BF16), before, preferred_element_type=F32)
        return jnp.where(named > 0, rank + float(first), -1.0), gate

    def joined(groups):
        pairs = [codes_of(p, i * cap) for i, p in enumerate(groups)]
        return [jnp.concatenate(parts, axis=1) for parts in zip(*pairs)]

    def build(s, codes, tokens_in, height):
        code, gate = codes
        row = lax.broadcasted_iota(jnp.int32, (height, code.shape[1]), 0).astype(F32)
        hit = code[s : s + 1, :] == row
        scale = jnp.sum(jnp.where(hit, gate[s : s + 1, :], 0.0), axis=1, keepdims=True)
        chosen_rows = jnp.dot(hit.astype(BF16), tokens_in, preferred_element_type=F32)
        return (chosen_rows * scale).astype(BF16)

    def pair_send(k, source, target):
        send(
            remote(
                source.at[1 - x], target, pair_sem.at[0, k], pair_sem.at[1, k], (z * 2 + (1 - x), g)
            )
        )

    zp, line = lax.rem(z, near), z // near
    n_line = n_z // near

    def near_start(u):
        remote(
            part.at[u, x], part_in.at[u], pair_sem.at[0, u], pair_sem.at[1, u], (z * 2 + (1 - x), g)
        ).wait_recv()
        pair_sum[u] = (part[u, x].astype(F32) + part_in[u].astype(F32)).astype(BF16)
        if near == 2:
            send(
                remote(
                    pair_sum.at[u, 1 - zp],
                    near_in.at[u],
                    near_sem.at[0, u],
                    near_sem.at[1, u],
                    ((line * 2 + (1 - zp)) * 2 + x, g),
                )
            )

    def finished_line(u, i):
        return lax.rem(y + n_y - u // CHUNKS, n_y) * steps + i

    def far_copy(u, i):
        to = finished_line(u, i)
        apart = lax.rem(to + n_line - line, n_line)
        return remote(
            near_sum.at[u, 0, i],
            far_in.at[u % CHUNKS, apart - 1],
            far_sem.at[0, u, i],
            far_sem.at[1, u % CHUNKS, apart],
            ((to * near + zp) * 2 + x, g),
        )

    def far_start(u):
        if near == 2:
            remote(
                pair_sum.at[u, zp],
                near_in.at[u],
                near_sem.at[0, u],
                near_sem.at[1, u],
                ((line * 2 + (1 - zp)) * 2 + x, g),
            ).wait_recv()
            near_sum[u, 0] = (pair_sum[u, zp].astype(F32) + near_in[u].astype(F32)).astype(BF16)
        else:
            near_sum[u, 0] = pair_sum[u, 0]
        for i in range(steps):

            @pl.when(finished_line(u, i) != line)
            def _():
                far_copy(u, i).start()

    def spread_copy(k, j):
        return remote(
            total.at[k],
            gathered.at[k, g],
            spread_sem.at[0, k, j],
            spread_sem.at[1, k, j],
            (d, lax.rem(g + j, n_ex)),
        )

    def finish(u):
        k = u % CHUNKS
        for i in range(steps):

            @pl.when(finished_line(u, i) == line)
            def _():
                result = near_sum[u, 0, i].astype(F32)
                for apart in range(1, n_line):
                    source = lax.rem(line + n_line - apart, n_line)
                    remote(
                        near_sum.at[u, 0, i],
                        far_in.at[k, apart - 1],
                        far_sem.at[0, u, i],
                        far_sem.at[1, k, apart],
                        ((source * near + zp) * 2 + x, g),
                    ).wait_recv()
                    result = result + far_in[k, apart - 1].astype(F32)
                total[k] = result.astype(BF16)
                gathered[k, g] = total[k]
                for j in range(1, n_ex):
                    spread_copy(k, j).start()

    def multiply(o):
        first = lax.rem(y + n_y - o, n_y) * 2
        codes = joined([first, first + 1])
        tokens_in = grads[pl.ds(first, 2)].reshape(2 * tok, columns)
        for s in range(local):
            picked[s] = build(s, codes, tokens_in, part_rows)
        for k in range(CHUNKS):
            u = o * CHUNKS + k
            if o == 0:
                loads[k].wait()
            for s in range(local):
                product[...] = lax.dot_general(
                    picked[s],
                    weights[s, k * width : (k + 1) * width, :],
                    (((1,), (1,)), ((), ())),
                    preferred_element_type=F32,
                )
                for t in range(n_dp // n_y):
                    stage[t, s * piece : (s + 1) * piece, :] = product[t * piece : (t + 1) * piece, :]
            for t in range(n_dp // n_y):
                part[u, t % 2, t // 2 % near, t // 2 // near] = stage[t].astype(BF16)
            pair_send(u, part.at[u], part_in.at[u])
            if u >= CHUNKS:
                near_start(u - CHUNKS)

    own[4].wait()
    gather_end(grad_ref, grads, grad_sem, grad_pair_sem, range(1))
    multiply(0)
    gather_forward(grad_ref, grads, grad_sem, grad_pair_sem)
    gather_start(shared_ref, shareds, shared_sem, shared_pair_sem)
    for k in range(1, n_ex):
        peer = lax.rem(g + k, n_ex)
        send(
            remote(
                hidden_piece(peer), hiddens.at[g], hidden_sem.at[0, k], hidden_sem.at[1, k], (d, peer)
            )
        )
    for o in range(1, n_y):
        gather_end(grad_ref, grads, grad_sem, grad_pair_sem, range(o, o + 1))
        multiply(o)
    all_tokens = grads[...].reshape(tokens, columns)
    all_codes = joined(range(n_ex))

    gather_forward(shared_ref, shareds, shared_sem, shared_pair_sem)
    gather_end(shared_ref, shareds, shared_sem, shared_pair_sem)
    own[5].wait()
    units = shared_ref.shape[0] * n_ex
    shared_all = shareds[...].reshape(units, columns)
    share = units // n_dp
    own_tokens = grads[g]
    for t in range(n_dp):
        spart[t % 2, t // 2] = lax.dot_general(
            own_tokens,
            shared_all[t * share : (t + 1) * share, :],
            (((1,), (1,)), ((), ())),
            preferred_element_type=F32,
        ).astype(BF16)
    pair_send(units_sent, spart, spart_in)

    def ring_start(k, own, arrived, sums, landing):
        remote(
            own.at[x], arrived, pair_sem.at[0, k], pair_sem.at[1, k], (z * 2 + (1 - x), g)
        ).wait_recv()
        sums[...] = (own[x].astype(F32) + arrived[...].astype(F32)).astype(BF16)
        for step in range(1, n_z):
            to = lax.rem(z + step, n_z)
            send(
                remote(
                    sums.at[to],
                    landing.at[step - 1],
                    ring_sem.at[0, step],
                    ring_sem.at[1, step],
                    (to * 2 + x, g),
                )
            )

    def ring_end(sums, landing):
        result = sums[z].astype(F32)
        for step in range(1, n_z):
            source = lax.rem(z + n_z - step, n_z)
            remote(
                sums.at[z],
                landing.at[step - 1],
                ring_sem.at[0, step],
                ring_sem.at[1, step],
                (source * 2 + x, g),
            ).wait_recv()
            result = result + landing[step - 1].astype(F32)
        return result.astype(BF16)

    own[6].wait()
    own[7].wait()
    stores = []

    def expert_weight_grad(s):
        expert_grad[s] = lax.dot_general(
            saved[s], rows[s], (((0,), (0,)), ((), ())), preferred_element_type=F32
        ).astype(BF16)
        stores.append(pltpu.make_async_copy(expert_grad.at[s], expert_grad_hbm.at[s], out_sem.at[s]))
        stores[-1].start()

    early, late = range(units_sent - CHUNKS), range(units_sent - CHUNKS, units_sent)
    for u in early:
        far_start(u)
    for s in range(local):
        rows[s] = build(local + s, all_codes, all_tokens, slot_rows)
    expert_weight_grad(0)
    for u in late:
        near_start(u)
    expert_weight_grad(1)
    for u in early:
        finish(u)
    for u in late:
        far_start(u)
    ring_start(units_sent, spart, spart_in, spair_sum, sring_in)
    for u in late:
        finish(u)
    for s in range(2, local):
        expert_weight_grad(s)
    for j in range(1, n_ex):
        source = lax.rem(g + n_ex - j, n_ex)
        remote(
            hidden_piece(source),
            hiddens.at[source],
            hidden_sem.at[0, j],
            hidden_sem.at[1, j],
            (d, source),
        ).wait_recv()
    weight_grad_ref[...] = lax.dot_general(
        hiddens[...].reshape(tokens, unit),
        all_tokens,
        (((0,), (0,)), ((), ())),
        preferred_element_type=F32,
    ).astype(BF16)
    hidden_grad_ref[...] = ring_end(spair_sum, sring_in)

    def labelled(shape, axis, listing, first):
        place = lax.broadcasted_iota(jnp.int32, shape, axis)
        label, offset = jnp.zeros(shape, jnp.int32), place
        for q in range(local):
            inside = place >= q * piece
            label = jnp.where(inside, listing[first + q], label)
            offset = jnp.where(inside, place - q * piece, offset)
        return label, offset

    packed = local * piece
    wanted, high = labelled((packed, packed), 0, new_ref, g * local)
    choices = []
    for p in range(n_ex):
        held, wide = labelled((packed, packed), 1, old_ref, p * local)
        choices.append(jnp.where((wanted == held) & (high == wide), 1.0, 0.0).astype(BF16))
    for k in range(CHUNKS):
        for j in range(1, n_ex):
            source = lax.rem(g + n_ex - j, n_ex)
            remote(
                total.at[k],
                gathered.at[k, source],
                spread_sem.at[0, k, j],
                spread_sem.at[1, k, j],
                (d, source),
            ).wait_recv()
        found = jnp.zeros((packed, width), F32)
        for p in range(n_ex):
            found = found + jnp.dot(choices[p], gathered[k, p], preferred_element_type=F32)
        routed_ref[:, k * width : (k + 1) * width] = found.astype(BF16)

    for copy in stores:
        copy.wait()
    for copy in sent:
        copy.wait_send()
    for k in range(CHUNKS):
        for j in range(1, n_ex):
            spread_copy(k, j).wait_send()
    for u in range(units_sent):
        for i in range(steps):

            @pl.when(finished_line(u, i) != line)
            def _():
                far_copy(u, i).wait_send()


def on_device(
    n_dp,
    n_ex,
    grad_output,
    gate_probs,
    routing,
    old_weights,
    old_slot_expert,
    new_slot_expert,
    saved_hidden,
    shared_hidden,
    shared_weight,
):
    local, hidden, columns = old_weights.shape
    slot_rows = saved_hidden.shape[1]
    tok, chosen = routing.shape
    units_here = shared_weight.shape[0]
    units = shared_hidden.shape[1]
    sliced = units_here % 128 == 0
    if not sliced:
        shared_hidden = shared_hidden.reshape(tok, n_ex, units_here).transpose(1, 0, 2)
    piece = slot_rows // n_dp
    packed = local * piece
    width = hidden // CHUNKS
    share = units // n_dp
    n_z, n_y = n_dp // 2, n_ex // 2
    ends = n_dp // n_y // 2
    near = 2 if ends % 2 == 0 else 1
    steps = ends // near
    units_sent = n_y * CHUNKS
    vmem = pl.BlockSpec(memory_space=pltpu.VMEM)
    anywhere = pl.BlockSpec(memory_space=pl.ANY)
    sem = pltpu.SemaphoreType.DMA
    expert_weight_grad, routed, hidden_grad, weight_grad = pl.pallas_call(
        functools.partial(exchange_kernel, n_dp, n_ex, sliced),
        out_shape=(
            jax.ShapeDtypeStruct((local, hidden, columns), BF16),
            jax.ShapeDtypeStruct((packed, hidden), BF16),
            jax.ShapeDtypeStruct((tok, share), BF16),
            jax.ShapeDtypeStruct((units_here, columns), BF16),
        ),
        in_specs=[anywhere] * 9,
        out_specs=(anywhere, vmem, vmem, vmem),
        scratch_shapes=[
            pltpu.SMEM(old_slot_expert.shape, jnp.int32),
            pltpu.SMEM(new_slot_expert.shape, jnp.int32),
            pltpu.VMEM((local, hidden, columns), BF16),
            pltpu.VMEM(saved_hidden.shape, BF16),
            pltpu.VMEM((local, hidden, columns), BF16),
            pltpu.VMEM((local, slot_rows, columns), BF16),
            pltpu.VMEM((n_ex, tok, columns), BF16),
            pltpu.VMEM((n_ex, chosen, tok), jnp.int32),
            pltpu.VMEM((n_ex, chosen, tok), F32),
            pltpu.VMEM((n_ex, tok, units_here), BF16),
            pltpu.VMEM((n_ex, units_here, columns), BF16),
            pltpu.VMEM((local, slot_rows // n_y, columns), BF16),
            pltpu.VMEM((slot_rows // n_y, width), F32),
            pltpu.VMEM((n_dp // n_y, packed, width), F32),
            pltpu.VMEM((units_sent, 2, near, steps, packed, width), BF16),
            pltpu.VMEM((units_sent, near, steps, packed, width), BF16),
            pltpu.VMEM((units_sent, near, steps, packed, width), BF16),
            pltpu.VMEM((units_sent, steps, packed, width), BF16),
            pltpu.VMEM((units_sent, 1, steps, packed, width), BF16),
            pltpu.VMEM((CHUNKS, n_z // near - 1, packed, width), BF16),
            pltpu.VMEM((CHUNKS, packed, width), BF16),
            pltpu.VMEM((CHUNKS, n_ex, packed, width), BF16),
            pltpu.VMEM((2, n_z, tok, share), BF16),
            pltpu.VMEM((n_z, tok, share), BF16),
            pltpu.VMEM((n_z, tok, share), BF16),
            pltpu.VMEM((n_z - 1, tok, share), BF16),
            sem((CHUNKS,)),
            sem((8,)),
            sem((local,)),
            sem((2, n_ex)),
            sem((2, n_ex)),
            sem((2, n_y)),
            sem((2, n_y)),
            sem((2, n_y)),
            sem((2, n_y)),
            sem((2, n_ex)),
            sem((2, units_sent + 1)),
            sem((2, units_sent)),
            sem((2, units_sent, max(steps, n_z // near))),
            sem((2, n_z)),
            sem((2, CHUNKS, n_ex)),
        ],
        compiler_params=pltpu.CompilerParams(
            collective_id=0, has_side_effects=True, vmem_limit_bytes=60 * 1024 * 1024
        ),
    )(
        grad_output,
        routing.T,
        gate_probs.T,
        old_slot_expert,
        new_slot_expert,
        shared_hidden,
        shared_weight,
        old_weights,
        saved_hidden,
    )
    routed = routed.reshape(local, piece, hidden)
    return expert_weight_grad, routed, hidden_grad, weight_grad


def solution(mesh):
    return jax.shard_map(
        functools.partial(on_device, mesh.shape["dp"], mesh.shape["expert"]),
        mesh=mesh,
        in_specs=(
            P("expert", "dp"),
            P("expert", None),
            P("expert", None),
            P("expert", None, "dp"),
            P(),
            P(),
            P("expert", None, None),
            P("expert", None),
            P("expert", "dp"),
        ),
        out_specs=(
            P("expert", None, "dp"),
            P("expert", "dp", None),
            P("expert", "dp"),
            P("expert", "dp"),
        ),
        check_vma=False,
    )
```
